128 devices in a mesh: grp: 4 (over x), dev: 32 (over y, z, core).
Axes of the slice: x: 4, y: 4, z: 4, core: 2. Of those that a mesh axis runs over, the one named last changes fastest.
Arguments:
- strength: bfloat16 [16384, 2, 120, 120], P(('grp', 'dev')), may hold values from -20 to 20
- freqs: float32 [16384, 3, 120], P(('grp', 'dev')), may hold values from 0.6 to 4.6
- owner: int32 [16384, 1], P(('grp', 'dev')), may hold values from 0 to 127; in each aligned block of 128 rows (0 to 127, 128 to 255, ...) at most 2 rows name the same one
- tile_slot: int32 [16384], P(('grp', 'dev')), may hold values from 0 to 127
- live_count: int32 [128], P(('grp', 'dev')), may hold values from 1 to 128, 14336 in all
Outputs:
- collision: float32 [128, 120, 4, 32, 120], P('grp', None, None, 'dev')
The draws below stay inside these ranges and needn't reach their ends.
Inputs may be any that keep to these rules, and one draw needn't show every extreme that they name: Among the live triplets of one device at most 2 name one owner; some owner is named by exactly 2 rows of some device. `live_count`: some device has all 128 slots live.
All inputs are finite; a program needn't handle non-finite values.
Results may differ from the reference program's by a relative error of at most 0.0046.
Values may be sent and summed in bfloat16 or wider, within the bound.
A program may use at most 128 MiB of HBM per device.

```python
import math
import jax
import jax.numpy as jnp
import numpy as np
from jax import lax

B = 120
TRIP = 128
TRIPLETS = 16384
CAP = 2
N_GRP = 4
N_DEV = 32
DEVICES = 128


def frequency_table(key, exponent):
    lower_key, upper_key, choose_key, third_key = jax.random.split(key, 4)
    shape = (TRIPLETS, 3, B)
    lower_band = 0.6 + 0.8 * jax.random.uniform(lower_key, shape, jnp.float32) ** exponent
    upper_band = 4.2 + 0.4 * jax.random.uniform(upper_key, shape, jnp.float32) ** 1.0
    third_band = 0.6 + 2.4 * jax.random.uniform(third_key, shape, jnp.float32) ** exponent
    chosen_ids = jax.random.randint(choose_key, (TRIPLETS, 3, 3), 0, B)
    lane_ids = jnp.arange(B, dtype=jnp.int32)
    chosen = jnp.any(chosen_ids[:, :, :, None] == lane_ids[None, None, None, :], axis=2)
    first_two = jnp.arange(3, dtype=jnp.int32)[None, :, None] < 2
    paired = jnp.where(chosen, upper_band, lower_band)
    return jnp.where(first_two, paired, third_band)


def draw_freqs(key, part):
    return frequency_table(key, 1.0)


def draw_strength(key, part):
    table = frequency_table(key, 1.0)
    key = jax.random.fold_in(key, 7)
    base_key = jax.random.fold_in(key, 0)
    spread = 0.6 * B ** (-0.25)
    shape = (TRIPLETS, 2, B, B)
    base = spread * jax.random.truncated_normal(base_key, -6.0, 6.0, shape, jnp.float32)
    boost = 2.0 * jnp.sinh(0.5 * table[:, :2, :])
    return (base * boost[:, :, :, None]).astype(jnp.bfloat16)


def set_ends(entries, rng, smallest, top_value):
    spot = [jax.random.randint(jax.random.fold_in(rng, axis), (), 0, length) for axis, length in enumerate(entries.shape)]
    main_axis = entries.shape.index(max(entries.shape))
    beside = spot[:main_axis] + [(spot[main_axis] + 1) % entries.shape[main_axis]] + spot[main_axis + 1:]
    return entries.at[tuple(spot)].set(smallest).at[tuple(beside)].set(top_value)


def split_up(count, total, reach, lean):
    weights = [(1 << 20) // math.isqrt(grade ** lean) + 1 for grade in range(2, count + 1)]
    surplus, counts = total - reach - (count - 1), [1] * (count - 1)
    while surplus > 0:
        free = [i for i in range(count - 1) if counts[i] < reach]
        mass, budget = sum([weights[i] for i in free]), surplus
        for i in free:
            extra = min(reach - counts[i], max(1, budget * weights[i] // mass), surplus)
            counts[i] = counts[i] + extra
            surplus = surplus - extra
    return np.array([reach] + counts)


def ragged_sizes(own_key, count, total, limit, lean):
    if count == 2:
        one = jax.random.randint(own_key, (), max(1, total - limit), min(limit, total - 1) + 1)
        return jnp.stack([one, total - one])
    tallies = jnp.asarray(split_up(count, total, limit, lean), jnp.int32)
    couples = (count - 1) // 2
    giver, sink = tallies[1:1 + 2 * couples:2], tallies[2:2 + 2 * couples:2]
    slack = jnp.minimum(giver - 1, limit - sink)
    moved = jax.random.randint(jax.random.fold_in(own_key, 1), (couples,), 0, 1 << 20) % (slack + 1)
    tallies = tallies.at[1:1 + 2 * couples:2].set(giver - moved).at[2:2 + 2 * couples:2].set(sink + moved)
    return tallies[jax.random.permutation(jax.random.fold_in(own_key, 2), count)]


def shared_out(stream_key, own, number, rows, count, top, reach, skew):
    ranking = jax.random.permutation(stream_key, count)
    packed, common = load_shares(count, rows * top, reach, skew, True), load_shares(count, rows * top, reach, skew, False)
    places = jnp.arange(count)

    def named(sizes, turn):
        used = int((sizes > 0).sum())
        fixed = max(1, used // 4)
        passed = fixed + (places - fixed + turn * (used - fixed)) % max(1, count - fixed)
        return jnp.zeros((count,), jnp.int32).at[ranking[jnp.where(places < fixed, places, passed)]].set(jnp.asarray(sizes, jnp.int32))

    sizes = jnp.where(number % 4 == 0, named(packed, number // 4), named(common, number - number // 4 - 1))
    mixed = jax.random.permutation(jax.random.fold_in(own, 3), count)
    source_of, receiver = mixed[0:count // 2 * 2:2], mixed[1:count // 2 * 2:2]
    slack = jnp.minimum(sizes[source_of] - 1, reach - sizes[receiver]) // 2
    slack = jnp.where((source_of == ranking[0]) | (receiver == ranking[0]) | (sizes[receiver] == 0), 0, jnp.maximum(slack, 0))
    passed = jax.random.randint(jax.random.fold_in(own, 4), (count // 2,), 0, 1 << 20) % (slack + 1)
    sizes = sizes.at[source_of].add(-passed).at[receiver].add(passed)
    members = jnp.searchsorted(jnp.cumsum(sizes), jnp.arange(rows * top), side="right").astype(jnp.int32)
    grid = members.reshape(top, rows).T
    grid = grid[jax.random.permutation(jax.random.fold_in(own, 1), rows)]
    turn = jax.random.randint(jax.random.fold_in(own, 2), (rows, 1), 0, top)
    return jnp.take_along_axis(grid, (jnp.arange(top)[None, :] + turn) % top, axis=1)


def load_shares(amount, total, most, lean, full):
    weights = [(1 << 20) // math.isqrt(standing ** lean) + 1 for standing in range(1, amount + 1)]
    largest = most if full else min(most, max(-(-total // amount), total * weights[0] // sum(weights)))
    least = 1 if total - largest >= amount - 1 else 0
    holding, spare = [largest] + [least] * (amount - 1), total - largest - least * (amount - 1)
    while spare > 0:
        movable = [i for i in range(1, amount) if holding[i] < largest] or [i for i in range(1, amount) if holding[i] < most]
        pool, budget = sum([weights[i] for i in movable]), spare
        for i in movable:
            extra = min(most - holding[i], max(1, budget * weights[i] // pool), spare)
            holding[i] = holding[i] + extra
            spare = spare - extra
    return np.array(holding)


def setup_inputs(seed: int = 0) -> dict:
    arg_keys = jax.random.split(jax.random.key(seed), 6)
    strength = draw_strength(jax.random.fold_in(arg_keys[5], 71), 0)
    freqs = draw_freqs(jax.random.fold_in(arg_keys[5], 71), 0)
    owner_keys = jax.random.split(jax.random.fold_in(arg_keys[2], 1), TRIPLETS // TRIP)
    owner_turns = jax.random.permutation(jax.random.fold_in(arg_keys[2], 3), TRIPLETS // TRIP)
    owner = jax.vmap(lambda own, number: shared_out(jax.random.fold_in(arg_keys[2], 2), own, number, TRIP, DEVICES, 1, CAP, 2))(owner_keys, owner_turns).reshape((TRIPLETS, 1))
    tile_slot = set_ends(jax.random.randint(arg_keys[3], (TRIPLETS,), 0, DEVICES), jax.random.fold_in(arg_keys[3], 1), 0, DEVICES - 1).astype(jnp.int32)
    live_count = ragged_sizes(arg_keys[4], DEVICES, DEVICES * TRIP * 7 // 8, TRIP, 2).astype(jnp.int32)
    return dict(strength=strength, freqs=freqs, owner=owner, tile_slot=tile_slot, live_count=live_count)


def reference(strength, freqs, owner, tile_slot, live_count):
    devices = N_GRP * N_DEV
    q_total = devices
    strength_d = strength.reshape(devices, TRIP, 2, B, B)
    freqs_d = freqs.reshape(devices, TRIP, 3, B)
    owner_d = owner.reshape(devices, TRIP)
    tile_d = tile_slot.reshape(devices, TRIP)

    def one_device(omega, inputs):
        strength_p, freqs_p, owner_p, tile_p, count_p = inputs
        occ = 1.0 / (jnp.exp(freqs_p) - 1.0)
        rowf = jnp.sqrt(occ[:, 0] * (occ[:, 0] + 1.0))
        colf = jnp.sqrt(occ[:, 1] * (occ[:, 1] + 1.0))
        third = occ[:, 2] + 1.0
        scaled = (strength_p[:, 0].astype(jnp.float32) * third[:, None, :]).astype(jnp.bfloat16)
        core = jnp.einsum('tjk,tlk->tjl', scaled.astype(jnp.float32), strength_p[:, 1].astype(jnp.float32))
        diff = freqs_p[:, 0, :, None] - freqs_p[:, 1, None, :]
        block = (rowf[:, :, None] * colf[:, None, :] * jnp.exp(-diff * diff / 0.5) * core).astype(jnp.bfloat16)
        live = jnp.arange(TRIP, dtype=jnp.int32) < count_p
        block_f = jnp.where(live[:, None, None], block.astype(jnp.float32), 0.0)
        grp_of = owner_p // N_DEV
        dev_of = owner_p % N_DEV
        rows = grp_of * N_DEV + tile_p // N_GRP
        cols = dev_of + N_DEV * (tile_p % N_GRP)
        omega = omega.at[rows, :, cols, :].add(block_f)
        return (omega, None)
    start = jnp.zeros((q_total, B, q_total, B), jnp.float32)
    omega, _ = lax.scan(one_device, start, (strength_d, freqs_d, owner_d, tile_d, live_count))
    rounded = lax.optimization_barrier(omega.astype(jnp.bfloat16)).astype(jnp.float32)
    sym = 0.5 * (rounded + rounded.transpose(2, 3, 0, 1))
    return sym.reshape(q_total, B, N_GRP, N_DEV, B)
```

```python
import functools

import jax
import jax.numpy as jnp
import numpy as np
from jax import lax
from jax.experimental import pallas as pl
from jax.experimental.pallas import tpu as pltpu
from jax.sharding import PartitionSpec as P

MESH = pl.DeviceIdType.MESH
LANES = 128
VMEM_BYTES = 56 * 2**20


def offsets_in_balanced_order():
    every = [
        (a, b, c, k) for a in range(4) for b in range(4) for c in range(4) for k in range(2)
    ][1:]
    seen, groups = set(), []
    for first in every:
        if first in seen:
            continue
        group, o = [], first
        for _ in range(3):
            for q in (o, tuple((4 - v) % 4 for v in o[:3]) + (o[3],)):
                if q not in group:
                    group.append(q)
            o = (o[1], o[2], o[0], o[3])
        seen.update(group)
        groups.append(group)
    order = np.random.RandomState(0).permutation(len(groups))
    return [o for g in order for o in groups[g]]


def position():
    g, d = lax.axis_index("grp"), lax.axis_index("dev")
    return g, d // 8, lax.rem(d // 2, 4), lax.rem(d, 2)


def at_offset(pos, off):
    x, y, z, core = pos
    dest_g = lax.rem(x + off[0], 4)
    dest_d = (lax.rem(y + off[1], 4) * 4 + lax.rem(z + off[2], 4)) * 2 + lax.rem(core + off[3], 2)
    return dest_g, dest_d


def enter(pos, offsets):
    barrier = pltpu.get_barrier_semaphore()
    for off in offsets:
        pl.semaphore_signal(
            barrier, inc=1, device_id=at_offset(pos, off), device_id_type=MESH
        )
    pl.semaphore_wait(barrier, len(offsets))


def exchange_kernel(offsets, width, by_tile, src, dst, send_sem, recv_sem, own_sem):
    pos = position()
    g, d = lax.axis_index("grp"), lax.axis_index("dev")
    n_dev = lax.axis_size("dev")
    n_grp = lax.axis_size("grp")
    me = d * n_grp + g if by_tile else g * n_dev + d
    enter(pos, offsets)
    own = pltpu.make_async_copy(
        src.at[pl.ds(me * width, width)], dst.at[pl.ds(me * width, width)], own_sem
    )
    own.start()
    for off in offsets:
        dest_g, dest_d = at_offset(pos, off)
        other = dest_d * n_grp + dest_g if by_tile else dest_g * n_dev + dest_d
        pltpu.make_async_remote_copy(
            src_ref=src.at[pl.ds(other * width, width)],
            dst_ref=dst.at[pl.ds(me * width, width)],
            send_sem=send_sem,
            recv_sem=recv_sem,
            device_id=(dest_g, dest_d),
            device_id_type=MESH,
        ).start()
    rest = pl.ds(0, len(offsets) * width)
    pltpu.make_async_copy(src.at[rest], src.at[rest], send_sem).wait()
    pltpu.make_async_copy(dst.at[rest], dst.at[rest], recv_sem).wait()
    own.wait()


def exchange(blocks, width, by_tile, collective_id, name):
    offsets = offsets_in_balanced_order()
    return pl.pallas_call(
        functools.partial(exchange_kernel, offsets, width, by_tile),
        name=name,
        out_shape=jax.ShapeDtypeStruct(blocks.shape, blocks.dtype),
        in_specs=[pl.BlockSpec(memory_space=pl.ANY)],
        out_specs=pl.BlockSpec(memory_space=pl.ANY),
        scratch_shapes=[pltpu.SemaphoreType.DMA] * 3,
        compiler_params=pltpu.CompilerParams(
            collective_id=collective_id, has_side_effects=True, vmem_limit_bytes=VMEM_BYTES
        ),
    )(blocks)


def blocks_kernel(
    cap, chunk, owner, tile, live, strength, freqs, out, s0, s1, rows, counts
):
    step = pl.program_id(0)
    steps = pl.num_programs(0)
    n_factor, _, bands, trip = strength.shape
    slots = out.shape[0] - 1

    eye = (
        lax.broadcasted_iota(jnp.int32, (trip, trip), 0)
        == lax.broadcasted_iota(jnp.int32, (trip, trip), 1)
    ).astype(jnp.bfloat16)

    @pl.when(step == 0)
    def _():
        occ = 1.0 / (jnp.exp(freqs[0]) - 1.0)
        rowf = jnp.sqrt(occ * (occ + 1.0))
        occ = 1.0 / (jnp.exp(freqs[1]) - 1.0)
        colf = jnp.sqrt(occ * (occ + 1.0))
        for q, value in enumerate((freqs[0], rowf, freqs[1], colf)):
            rows[pl.ds(q, trip, stride=8), 0:bands] = value.T

    third = 1.0 / (jnp.exp(freqs[2]) - 1.0) + 1.0
    for r in range(chunk):
        scaled = (strength[0, r].astype(jnp.float32) * third).astype(jnp.bfloat16)
        for value, store in ((scaled, s0), (strength[1, r], s1)):
            turned = lax.dot_general(
                eye, value, (((1,), (1,)), ((), ())), preferred_element_type=jnp.float32
            )
            store[pl.ds(step * chunk + r, trip, stride=bands), 0:bands] = turned

    @pl.when(step == steps - 1)
    def _():
        dead = jnp.full((16, LANES), -1.0, jnp.bfloat16)

        @pl.loop(0, slots)
        def _(s):
            out[s, 0:16, :] = dead

        @pl.loop(0, counts.shape[0])
        def _(s):
            counts[s] = 0

        lane = lax.broadcasted_iota(jnp.int32, (bands, LANES), 1)

        @pl.loop(0, trip, unroll=4)
        def _(t):
            target = owner[t]
            alive = t < live[0]
            before = counts[target]
            counts[target] = before + alive.astype(jnp.int32)
            place = jnp.where(alive, target * cap + before, slots)
            a = s0[pl.ds(t * bands, bands), 0:bands].astype(jnp.bfloat16)
            b = s1[pl.ds(t * bands, bands), 0:bands].astype(jnp.bfloat16)
            core = lax.dot_general(
                a, b, (((1,), (1,)), ((), ())), preferred_element_type=jnp.float32
            )
            line = rows[pl.ds(pl.multiple_of(t * 8, 8), 8), :]
            column = line.T[0:bands]
            diff = column[:, 0:1] - line[2:3, 0:bands]
            scale = column[:, 1:2] * line[3:4, 0:bands] * jnp.exp(-diff * diff / 0.5)
            value = (scale * core).astype(jnp.bfloat16)
            value = jnp.concatenate(
                [value, jnp.zeros((bands, LANES - bands), jnp.bfloat16)], axis=1
            )
            label = tile[t].astype(jnp.float32).astype(jnp.bfloat16)
            out[place] = jnp.where(lane < bands, value, label)


def make_blocks(strength, freqs, owner, tile, live, cap, devices):
    trip, n_factor, bands, _ = strength.shape
    by_lane = strength.transpose(1, 2, 3, 0)
    freqs = freqs.transpose(1, 2, 0)
    chunk = 4
    smem = pl.BlockSpec(memory_space=pltpu.SMEM)
    return pl.pallas_call(
        functools.partial(blocks_kernel, cap, chunk),
        name="blocks",
        grid=(bands // chunk,),
        out_shape=jax.ShapeDtypeStruct((devices * cap + 1, bands, LANES), jnp.bfloat16),
        in_specs=[
            smem,
            smem,
            smem,
            pl.BlockSpec((n_factor, chunk, bands, trip), lambda i: (0, i, 0, 0)),
            pl.BlockSpec(memory_space=pltpu.VMEM),
        ],
        out_specs=pl.BlockSpec(memory_space=pltpu.VMEM),
        scratch_shapes=[
            pltpu.VMEM((trip * bands, LANES), jnp.float32),
            pltpu.VMEM((trip * bands, LANES), jnp.float32),
            pltpu.VMEM((trip * 8, LANES), jnp.float32),
            pltpu.SMEM((devices,), jnp.int32),
        ],
        compiler_params=pltpu.CompilerParams(vmem_limit_bytes=VMEM_BYTES),
    )(owner, tile, live, by_lane, freqs)


def sum_kernel(labels, got, out, total):
    step = pl.program_id(0)
    here = got.shape[0]

    @pl.when(step == 0)
    def _():
        @pl.loop(0, total.shape[0], unroll=4)
        def _(k):
            total[k] = jnp.zeros(total.shape[1:], jnp.float32)

    @pl.loop(0, here)
    def _(s):
        label = labels[step * here + s]

        @pl.when(label >= 0)
        def _():
            total[label] += got[s].astype(jnp.float32)

    @pl.when(step == pl.num_programs(0) - 1)
    def _():
        @pl.loop(0, total.shape[0], unroll=4)
        def _(k):
            out[k] = total[k].astype(out.dtype)


def sum_tiles(labels, got, tiles):
    slots, bands, lanes = got.shape
    here = 16
    return pl.pallas_call(
        sum_kernel,
        name="sum_tiles",
        grid=(slots // here,),
        out_shape=jax.ShapeDtypeStruct((tiles, bands, lanes), jnp.bfloat16),
        in_specs=[
            pl.BlockSpec(memory_space=pltpu.SMEM),
            pl.BlockSpec((here, bands, lanes), lambda i: (i, 0, 0)),
        ],
        out_specs=pl.BlockSpec(memory_space=pltpu.VMEM),
        scratch_shapes=[pltpu.VMEM((tiles, bands, lanes), jnp.float32)],
        compiler_params=pltpu.CompilerParams(vmem_limit_bytes=VMEM_BYTES),
    )(labels, got)


def symmetrize_kernel(n_grp, omega, partner, out):
    per, bands, lanes = omega.shape
    eye = (
        lax.broadcasted_iota(jnp.int32, (lanes, lanes), 0)
        == lax.broadcasted_iota(jnp.int32, (lanes, lanes), 1)
    ).astype(jnp.bfloat16)
    for k in range(per):
        turned = lax.dot_general(
            eye, partner[k], (((1,), (1,)), ((), ())), preferred_element_type=jnp.float32
        )
        value = 0.5 * (omega[k][:, 0:bands].astype(jnp.float32) + turned[0:bands])
        i, c = divmod(k, n_grp)
        out[i, pl.ds(c, bands, stride=n_grp), :] = value


def symmetrize(omega, partner, n_grp):
    tiles, bands, lanes = omega.shape
    rows = 2
    spec = pl.BlockSpec((rows * n_grp, bands, lanes), lambda i: (i, 0, 0))
    return pl.pallas_call(
        functools.partial(symmetrize_kernel, n_grp),
        name="symmetrize",
        grid=(tiles // (rows * n_grp),),
        out_shape=jax.ShapeDtypeStruct((tiles // n_grp, bands * n_grp, bands), jnp.float32),
        in_specs=[spec, spec],
        out_specs=pl.BlockSpec((rows, bands * n_grp, bands), lambda i: (i, 0, 0)),
        compiler_params=pltpu.CompilerParams(vmem_limit_bytes=VMEM_BYTES),
    )(omega, partner)


def per_device(strength, freqs, owner, tile_slot, live_count):
    trip, _, bands, _ = strength.shape
    n_grp = lax.axis_size("grp")
    n_dev = lax.axis_size("dev")
    devices = n_grp * n_dev
    cap = 2
    outgoing = make_blocks(
        strength, freqs, owner[:, 0], tile_slot, live_count, cap, devices
    )
    got = exchange(outgoing, cap, False, 1, "send_blocks")
    labels = got[:, 0, bands].astype(jnp.int32)
    omega = sum_tiles(labels, got, devices)
    partner = exchange(omega, 1, True, 2, "send_tiles")
    sym = symmetrize(omega, partner, n_grp)
    return sym.reshape(devices // n_grp, bands, n_grp, 1, bands)


def solution(mesh):
    return jax.shard_map(
        per_device,
        mesh=mesh,
        in_specs=(
            P(("grp", "dev"), None, None, None),
            P(("grp", "dev"), None, None),
            P(("grp", "dev"), None),
            P(("grp", "dev")),
            P(("grp", "dev")),
        ),
        out_specs=P("grp", None, None, "dev", None),
        check_vma=False,
    )
```

```python
import functools

import jax
import jax.numpy as jnp
from jax import lax
from jax.experimental import pallas as pl
from jax.experimental.pallas import tpu as pltpu
from jax.sharding import PartitionSpec as P

MESH = pl.DeviceIdType.MESH
LANES = 128
SIDE = 4
VMEM_BYTES = 56 * 2**20


def position():
    g, d = lax.axis_index("grp"), lax.axis_index("dev")
    return g, d // 8, lax.rem(d // 2, 4), lax.rem(d, 2)


def device_at(pos, axis, step, flip):
    at = list(pos)
    if step:
        at[axis] = lax.rem(pos[axis] + step, SIDE)
    if flip:
        at[3] = 1 - pos[3]
    return at[0], (at[1] * SIDE + at[2]) * 2 + at[3]


def exchange_kernel(places, n, *refs):
    srcs, dsts, firsts, seconds = (refs[k * n : (k + 1) * n] for k in range(4))
    send_sem, recv_sem, own_sem = refs[4 * n :]
    pos = position()
    moves = [[(r, False) for r in (1, 3, 2)]] * 2 + [
        [(r, f) for r in (1, 3, 2) for f in (False, True)] + [(0, True)]
    ]

    barrier = pltpu.get_barrier_semaphore()
    greeted = [(a, r, f) for a in range(3) for r in (1, 2, 3) for f in (False, True)]
    greeted.append((0, 0, True))
    for a, r, f in greeted:
        pl.semaphore_signal(
            barrier, inc=1, device_id=device_at(pos, a, r, f), device_id_type=MESH
        )
    pl.semaphore_wait(barrier, len(greeted))

    def view(ref, whole, p, axis, at, core):
        index = [slice(None)] * 4
        index[places[axis]] = at
        if core is not None:
            index[places[3]] = core
        if whole:
            return ref.at[tuple(index) + (p,)]
        return ref.at[(p,) + tuple(index)]

    def ends(k, stage, p, step, flip):
        axis = (p + stage) % 3
        last = stage == 2
        there = lax.rem(pos[axis] + step, SIDE) if step else pos[axis]
        other = (1 - pos[3] if flip else pos[3]) if last else None
        here = pos[3] if last else None
        source = (srcs, firsts, seconds)[stage][k]
        target = (firsts, seconds, dsts)[stage][k]
        return (
            view(source, stage == 0, p, axis, there, other),
            view(target, last, p, axis, pos[axis], here),
        )

    def own(k, stage, p):
        source, target = ends(k, stage, p, 0, False)
        return pltpu.make_async_copy(source, target, own_sem.at[k, stage, p])

    def remote(k, stage, p, m):
        step, flip = moves[stage][m]
        source, target = ends(k, stage, p, step, flip)
        return pltpu.make_async_remote_copy(
            src_ref=source,
            dst_ref=target,
            send_sem=send_sem.at[k, stage, p, m],
            recv_sem=recv_sem.at[k, stage, p, m],
            device_id=device_at(pos, (p + stage) % 3, step, flip),
            device_id_type=MESH,
        )

    for stage in range(3):
        jobs = [
            (k, stage, p) for p in range(3) for k in range(n) if p < firsts[k].shape[0]
        ]
        for m in range(len(moves[stage])):
            for job in jobs:
                remote(*job, m).start()
        for job in jobs:
            own(*job).start()
        for job in jobs:
            own(*job).wait()
            for m in range(len(moves[stage])):
                remote(*job, m).wait()


def exchange(arrays, places, collective_id, name):
    n = len(arrays)
    thirds = [
        pltpu.VMEM((a.shape[4],) + a.shape[:4] + a.shape[5:], a.dtype) for a in arrays
    ]
    anywhere = [pl.BlockSpec(memory_space=pl.ANY)] * n
    return pl.pallas_call(
        functools.partial(exchange_kernel, places, n),
        name=name,
        out_shape=[jax.ShapeDtypeStruct(a.shape, a.dtype) for a in arrays],
        in_specs=anywhere,
        out_specs=anywhere,
        scratch_shapes=thirds
        + thirds
        + [pltpu.SemaphoreType.DMA((n, 3, 3, 7))] * 2
        + [pltpu.SemaphoreType.DMA((n, 3, 3))],
        compiler_params=pltpu.CompilerParams(
            collective_id=collective_id, has_side_effects=True, vmem_limit_bytes=VMEM_BYTES
        ),
    )(*arrays)


def blocks_kernel(
    chunk, owner, tile, live, strength, freqs, out, labels, s0, s1, rows, counts
):
    step = pl.program_id(0)
    steps = pl.num_programs(0)
    n_factor, _, bands, trip = strength.shape
    cap = out.shape[2]

    eye = (
        lax.broadcasted_iota(jnp.int32, (trip, trip), 0)
        == lax.broadcasted_iota(jnp.int32, (trip, trip), 1)
    ).astype(jnp.bfloat16)

    @pl.when(step == 0)
    def _():
        occ = 1.0 / (jnp.exp(freqs[0]) - 1.0)
        rowf = jnp.sqrt(occ * (occ + 1.0))
        occ = 1.0 / (jnp.exp(freqs[1]) - 1.0)
        colf = jnp.sqrt(occ * (occ + 1.0))
        for q, value in enumerate((freqs[0], rowf, freqs[1], colf)):
            rows[pl.ds(q, trip, stride=8), 0:bands] = value.T

    third = 1.0 / (jnp.exp(freqs[2]) - 1.0) + 1.0
    for r in range(chunk):
        scaled = (strength[0, r].astype(jnp.float32) * third).astype(jnp.bfloat16)
        for value, store in ((scaled, s0), (strength[1, r], s1)):
            turned = lax.dot_general(
                eye, value, (((1,), (1,)), ((), ())), preferred_element_type=jnp.float32
            )
            store[pl.ds(step * chunk + r, trip, stride=bands), 0:bands] = turned

    @pl.when(step == steps - 1)
    def _():
        @pl.loop(0, counts.shape[0])
        def _(s):
            counts[s] = 0
            for r in range(cap):
                labels[s, r] = -1

        @pl.loop(0, trip, unroll=4)
        def _(t):
            target = owner[t]
            alive = t < live[0]
            before = counts[target]
            counts[target] = before + alive.astype(jnp.int32)
            a = s0[pl.ds(t * bands, bands), 0:bands].astype(jnp.bfloat16)
            b = s1[pl.ds(t * bands, bands), 0:bands].astype(jnp.bfloat16)
            core = lax.dot_general(
                a, b, (((1,), (1,)), ((), ())), preferred_element_type=jnp.float32
            )
            line = rows[pl.ds(pl.multiple_of(t * 8, 8), 8), :]
            column = line.T[0:bands]
            diff = column[:, 0:1] - line[2:3, 0:bands]
            scale = column[:, 1:2] * line[3:4, 0:bands] * jnp.exp(-diff * diff / 0.5)
            value = jnp.pad(scale * core, ((0, 0), (0, LANES - bands)))
            value = value.reshape(out.shape[1], out.shape[3], LANES).astype(out.dtype)

            @pl.when(alive)
            def _():
                out[target, :, before] = value
                labels[target, before] = tile[t]


def make_blocks(strength, freqs, owner, tile, live, cap, devices):
    trip, n_factor, bands, _ = strength.shape
    by_lane = strength.transpose(1, 2, 3, 0)
    freqs = freqs.transpose(1, 2, 0)
    chunk = 4
    smem = pl.BlockSpec(memory_space=pltpu.SMEM)
    return pl.pallas_call(
        functools.partial(blocks_kernel, chunk),
        name="blocks",
        grid=(bands // chunk,),
        out_shape=[
            jax.ShapeDtypeStruct((devices, 3, cap, bands // 3, LANES), jnp.bfloat16),
            jax.ShapeDtypeStruct((devices, LANES), jnp.int32),
        ],
        in_specs=[
            smem,
            smem,
            smem,
            pl.BlockSpec((n_factor, chunk, bands, trip), lambda i: (0, i, 0, 0)),
            pl.BlockSpec(memory_space=pltpu.VMEM),
        ],
        out_specs=[pl.BlockSpec(memory_space=pltpu.VMEM), smem],
        scratch_shapes=[
            pltpu.VMEM((trip * bands, LANES), jnp.float32),
            pltpu.VMEM((trip * bands, LANES), jnp.float32),
            pltpu.VMEM((trip * 8, LANES), jnp.float32),
            pltpu.SMEM((devices,), jnp.int32),
        ],
        compiler_params=pltpu.CompilerParams(vmem_limit_bytes=VMEM_BYTES),
    )(owner, tile, live, by_lane, freqs)


def sum_kernel(labels, got, out, total):
    step = pl.program_id(0)
    here, _, cap = got.shape[:3]

    @pl.when(step == 0)
    def _():
        @pl.loop(0, total.shape[0], unroll=4)
        def _(k):
            total[k] = jnp.zeros(total.shape[1:], jnp.float32)

    @pl.loop(0, here)
    def _(s):
        for r in range(cap):
            label = labels[step * here + s, r]

            @pl.when(label >= 0)
            def _():
                total[label] += got[s, :, r].astype(jnp.float32)

    @pl.when(step == pl.num_programs(0) - 1)
    def _():
        @pl.loop(0, total.shape[0], unroll=4)
        def _(k):
            out[k] = total[k].astype(out.dtype)


def sum_tiles(labels, got, tiles):
    devices, thirds, cap, part, lanes = got.shape
    here = 16
    return pl.pallas_call(
        sum_kernel,
        name="sum_tiles",
        grid=(devices // here,),
        out_shape=jax.ShapeDtypeStruct((tiles, thirds, part, lanes), jnp.bfloat16),
        in_specs=[
            pl.BlockSpec(memory_space=pltpu.SMEM),
            pl.BlockSpec((here, thirds, cap, part, lanes), lambda i: (i, 0, 0, 0, 0)),
        ],
        out_specs=pl.BlockSpec(memory_space=pltpu.VMEM),
        scratch_shapes=[pltpu.VMEM((tiles, thirds, part, lanes), jnp.float32)],
        compiler_params=pltpu.CompilerParams(vmem_limit_bytes=VMEM_BYTES),
    )(labels, got)


def symmetrize_kernel(n_grp, omega, partner, out):
    per, thirds, part, lanes = omega.shape
    bands = thirds * part
    eye = (
        lax.broadcasted_iota(jnp.int32, (lanes, lanes), 0)
        == lax.broadcasted_iota(jnp.int32, (lanes, lanes), 1)
    ).astype(jnp.bfloat16)
    for k in range(per):
        other = partner[k].astype(jnp.float32).reshape(bands, lanes).astype(jnp.bfloat16)
        turned = lax.dot_general(
            eye, other, (((1,), (1,)), ((), ())), preferred_element_type=jnp.float32
        )
        mine = omega[k].astype(jnp.float32).reshape(bands, lanes)
        i, c = divmod(k, n_grp)
        out[i, pl.ds(c, bands, stride=n_grp), :] = 0.5 * (mine[:, 0:bands] + turned[0:bands])


def symmetrize(omega, partner, n_grp):
    tiles, thirds, part, lanes = omega.shape
    bands = thirds * part
    rows = 2
    spec = pl.BlockSpec((rows * n_grp, thirds, part, lanes), lambda i: (i, 0, 0, 0))
    return pl.pallas_call(
        functools.partial(symmetrize_kernel, n_grp),
        name="symmetrize",
        grid=(tiles // (rows * n_grp),),
        out_shape=jax.ShapeDtypeStruct((tiles // n_grp, bands * n_grp, bands), jnp.float32),
        in_specs=[spec, spec],
        out_specs=pl.BlockSpec((rows, bands * n_grp, bands), lambda i: (i, 0, 0)),
        compiler_params=pltpu.CompilerParams(vmem_limit_bytes=VMEM_BYTES),
    )(omega, partner)


def per_device(strength, freqs, owner, tile_slot, live_count):
    trip, _, bands, _ = strength.shape
    n_grp = lax.axis_size("grp")
    n_dev = lax.axis_size("dev")
    devices = n_grp * n_dev
    cap = 2
    outgoing, labels = make_blocks(
        strength, freqs, owner[:, 0], tile_slot, live_count, cap, devices
    )
    part = (3, cap, bands // 3, LANES)
    by_grp = (n_grp, SIDE, SIDE, 2)
    got, got_labels = exchange(
        [outgoing.reshape(*by_grp, *part), labels.reshape(*by_grp, 1, 1, LANES)],
        (0, 1, 2, 3),
        1,
        "send_blocks",
    )
    omega = sum_tiles(
        got_labels.reshape(devices, LANES), got.reshape(devices, *part), devices
    )
    by_dev = (SIDE, SIDE, 2, n_grp)
    (partner,) = exchange(
        [omega.reshape(*by_dev, *omega.shape[1:])], (3, 0, 1, 2), 2, "send_tiles"
    )
    partner = partner.reshape(omega.shape)
    sym = symmetrize(omega, partner, n_grp)
    return sym.reshape(devices // n_grp, bands, n_grp, 1, bands)


def solution(mesh):
    return jax.shard_map(
        per_device,
        mesh=mesh,
        in_specs=(
            P(("grp", "dev"), None, None, None),
            P(("grp", "dev"), None, None),
            P(("grp", "dev"), None),
            P(("grp", "dev")),
            P(("grp", "dev")),
        ),
        out_specs=P("grp", None, None, "dev", None),
        check_vma=False,
    )
```

```python
import functools

import jax
import jax.numpy as jnp
from jax import lax
from jax.experimental import pallas as pl
from jax.experimental.pallas import tpu as pltpu
from jax.sharding import PartitionSpec as P

MESH = pl.DeviceIdType.MESH
LANES = 128
SIDE = 4
VMEM_BYTES = 56 * 2**20


PARTS = 3
WALK = 400


def position():
    g, d = lax.axis_index("grp"), lax.axis_index("dev")
    return g, d // 8, lax.rem(d // 2, 4), lax.rem(d, 2)


def device_at(pos, axis, step, flip):
    at = list(pos)
    if step:
        at[axis] = lax.rem(pos[axis] + step, SIDE)
    if flip:
        at[3] = 1 - pos[3]
    return at[0], (at[1] * SIDE + at[2]) * 2 + at[3]


def exchange_kernel(plans, *refs):
    n = len(plans)
    n_shared = sum(plan[2] for plan in plans)
    srcs, dsts, refs = refs[:n], refs[n : 2 * n], refs[2 * n :]
    shared_dsts, refs = refs[:n_shared], refs[n_shared:]
    firsts, seconds, refs = refs[:n], refs[n : 2 * n], refs[2 * n :]
    shared_in, refs = refs[:n_shared], refs[n_shared:]
    send_sem, recv_sem, own_sem = refs
    pos = position()

    barrier = pltpu.get_barrier_semaphore()
    greeted = [(a, r, f) for a in range(3) for r in (1, 2, 3) for f in (False, True)]
    greeted.append((0, 0, True))
    for a, r, f in greeted:
        pl.semaphore_signal(
            barrier, inc=1, device_id=device_at(pos, a, r, f), device_id_type=MESH
        )
    pl.semaphore_wait(barrier, len(greeted))

    def view(ref, places, front, p, axis, at, core):
        index = [slice(None)] * 4
        index[places[axis]] = at
        if core is not None:
            index[places[3]] = core
        return ref.at[(p,) + tuple(index)] if front else ref.at[tuple(index) + (p,)]

    def ends(k, stage, p, step, flip):
        src_places, dst_places, _ = plans[k]
        axis = (p + stage) % 3
        there = lax.rem(pos[axis] + step, SIDE) if step else pos[axis]
        if stage == 0:
            return (
                view(srcs[k], src_places, False, p, axis, there, None),
                view(firsts[k], src_places, True, p, axis, pos[axis], None),
            )
        if stage == 1:
            return (
                view(firsts[k], src_places, True, p, axis, there, None),
                view(seconds[k], src_places, True, p, axis, pos[axis], None),
            )
        if flip is None:
            index = [slice(None)] * 3
            index[axis] = pos[axis]
            return (
                view(seconds[k], src_places, True, p, axis, there, 2),
                shared_in[0].at[(p,) + tuple(index)],
            )
        core = 1 - pos[3] if flip else pos[3]
        return (
            view(seconds[k], src_places, True, p, axis, there, core),
            view(dsts[k], dst_places, False, p, axis, pos[axis], pos[3]),
        )

    def moves(k, stage):
        steps = (1, 3, 2)
        if stage < 2:
            return [(r, False) for r in steps]
        most = [(r, f) for r in steps for f in (False, True)] + [(0, True)]
        return ([(r, None) for r in steps] if plans[k][2] else []) + most

    def own(k, stage, p, shared=False):
        source, target = ends(k, stage, p, 0, None if shared else False)
        return pltpu.make_async_copy(source, target, own_sem.at[k, stage + shared, p])

    def remote(k, stage, p, m):
        step, flip = moves(k, stage)[m]
        source, target = ends(k, stage, p, step, flip)
        return pltpu.make_async_remote_copy(
            src_ref=source,
            dst_ref=target,
            send_sem=send_sem.at[k, stage, p, m],
            recv_sem=recv_sem.at[k, stage, p, m],
            device_id=device_at(pos, (p + stage) % 3, step, bool(flip)),
            device_id_type=MESH,
        )

    def pass_on(p):
        target = shared_dsts[0].at[:, :, :, pos[3], p]
        there = pltpu.make_async_remote_copy(
            src_ref=shared_in[0].at[p],
            dst_ref=target,
            send_sem=send_sem.at[0, 3, p, 0],
            recv_sem=recv_sem.at[0, 3, p, 0],
            device_id=device_at(pos, 0, 0, True),
            device_id_type=MESH,
        )
        return there, pltpu.make_async_copy(shared_in[0].at[p], target, own_sem.at[0, 4, p])

    def jobs(p):
        return [k for k in range(n) if p < firsts[k].shape[0]]

    def start(stage, p):
        for k in jobs(p):
            for m in range(len(moves(k, stage))):
                remote(k, stage, p, m).start()
            own(k, stage, p).start()
            if stage == 2 and plans[k][2]:
                own(k, stage, p, True).start()

    def arrive(stage, p, which=None):
        for k in jobs(p):
            for m, (_, flip) in enumerate(moves(k, stage)):
                if which is None or which == (flip is None):
                    remote(k, stage, p, m).wait_recv()
            if not which:
                own(k, stage, p).wait()
            if stage == 2 and plans[k][2] and which is not False:
                own(k, stage, p, True).wait()

    for p in range(PARTS):
        start(0, p)
    for stage in (1, 2):
        for p in range(PARTS):
            arrive(stage - 1, p)
            start(stage, p)
    if n_shared:
        for p in range(PARTS):
            arrive(2, p, True)
            for copy in pass_on(p):
                copy.start()
    for p in range(PARTS):
        arrive(2, p, False)
    if n_shared:
        for p in range(PARTS):
            there, here = pass_on(p)
            there.wait()
            here.wait()
    for p in range(PARTS):
        for stage in range(3):
            for k in jobs(p):
                for m in range(len(moves(k, stage))):
                    remote(k, stage, p, m).wait_send()


def exchange(arrays, plans, collective_id, name):
    n = len(arrays)
    outs, shared_outs, temps, shared_temps = [], [], [], []
    for a, (src_places, dst_places, shared) in zip(arrays, plans):
        front = [0] * 4
        for axis in range(4):
            front[dst_places[axis]] = 2 if axis == 3 else SIDE
        rest = a.shape[4:]
        outs.append(jax.ShapeDtypeStruct((*front, *rest), a.dtype))
        temps.append(pltpu.VMEM((rest[0],) + a.shape[:4] + rest[1:], a.dtype))
        if shared:
            shared_outs.append(jax.ShapeDtypeStruct((SIDE, SIDE, SIDE, 2, *rest), a.dtype))
            shared_temps.append(pltpu.VMEM((rest[0], SIDE, SIDE, SIDE) + rest[1:], a.dtype))
    outs = outs + shared_outs
    anywhere = pl.BlockSpec(memory_space=pl.ANY)
    return pl.pallas_call(
        functools.partial(exchange_kernel, plans),
        name=name,
        out_shape=outs,
        in_specs=[anywhere] * n,
        out_specs=[anywhere] * len(outs),
        scratch_shapes=temps
        + temps
        + shared_temps
        + [pltpu.SemaphoreType.DMA((n, 4, PARTS, 10))] * 2
        + [pltpu.SemaphoreType.DMA((n, 5, PARTS))],
        compiler_params=pltpu.CompilerParams(
            collective_id=collective_id, has_side_effects=True, vmem_limit_bytes=VMEM_BYTES
        ),
    )(*arrays)


def plan_dense(grid, owner, tile, n_live, labels, cell, place, flip, left):
    n_grp, n_dev = grid
    chips = n_grp * n_dev // 2

    @pl.loop(0, n_live)
    def _(t):
        o = owner[t]
        e = lax.rem(o, 2) * chips + lax.div(o, 2)
        r = (cell[e] >= 0).astype(jnp.int32)
        cell[e] = t
        place[t] = e + r * 2 * chips
        labels[o, r] = tile[t]


def plan_shared(grid, owner, tile, n_live, labels, cell, place, flip, left):
    n_grp, n_dev = grid
    devices = n_grp * n_dev
    chips = devices // 2

    def first(t, n):
        o = owner[t]
        e = lax.rem(o, 2) * chips + lax.div(o, 2)
        taken = cell[e] >= 0

        @pl.when(jnp.logical_not(taken))
        def _():
            cell[e] = t
            place[t] = e
            labels[o, 0] = tile[t]

        @pl.when(taken)
        def _():
            left[n] = t

        return n + taken.astype(jnp.int32)

    n_left = lax.fori_loop(0, n_live, first, jnp.int32(0))

    def insert(q, carry):
        lost, noise = carry

        def body(state):
            t, steps, noise = state
            o, k = owner[t], tile[t]
            x = lax.rem(k, n_grp) * n_dev + lax.div(k, n_grp)
            e0 = lax.rem(o, 2) * chips + lax.div(o, 2)
            e1 = devices + lax.div(o, 2)
            e2 = lax.rem(x, 2) * chips + lax.div(x, 2)
            e3 = devices + lax.div(x, 2)
            noise = lax.rem(noise * 1103 + 12345, 65521)
            pick = lax.rem(lax.div(noise, 8), 4)
            for r, e in ((3, e3), (2, e2), (0, e0), (1, e1)):
                pick = jnp.where(cell[e] < 0, r, pick)
            e = jnp.where(pick == 0, e0, jnp.where(pick == 1, e1, jnp.where(pick == 2, e2, e3)))
            turned = pick >= 2
            to = jnp.where(turned, x, o)
            label = jnp.where(turned, lax.rem(o, n_dev) * n_grp + lax.div(o, n_dev), k)
            victim = cell[e]
            cell[e] = t
            place[t] = e
            flip[t] = turned.astype(jnp.int32)
            both = (e >= devices).astype(jnp.int32)
            labels[to, both] = label

            @pl.when(e >= devices)
            def _():
                labels[to + 1 - 2 * lax.rem(to, 2), 1] = -1

            return victim, steps + 1, noise

        t, _, noise = lax.while_loop(
            lambda state: (state[0] >= 0) & (state[1] < WALK), body, (left[q], 0, noise)
        )
        return lost | (t >= 0).astype(jnp.int32), noise

    lost, _ = lax.fori_loop(0, n_left, insert, (jnp.int32(0), jnp.int32(1)))

    @pl.when(lost > 0)
    def _():
        @pl.loop(0, devices)
        def _(o):
            labels[o, 2] = 1


def blocks_kernel(
    grid, plan, group, owner, tile, live, strength, freqs, out, labels,
    here, turned, rows, block, cell, place, flip, left, in_sem, out_sem,
):
    _, bands, _, trip = strength.shape
    devices = grid[0] * grid[1]
    pieces = in_sem.shape[0]
    piece = bands // pieces

    def fetch(i):
        part = pl.ds(i * piece, piece)
        return pltpu.make_async_copy(strength.at[:, part], here.at[:, part], in_sem.at[i])

    for i in range(pieces):
        fetch(i).start()

    @pl.loop(0, devices, unroll=8)
    def _(o):
        labels[o, 0] = -1
        labels[o, 1] = -1
        labels[o, 2] = 0

    @pl.loop(0, cell.shape[0], unroll=8)
    def _(e):
        cell[e] = -1

    @pl.loop(0, trip, unroll=8)
    def _(t):
        place[t] = -1
        flip[t] = 0

    plan(grid, owner, tile, live[0], labels, cell, place, flip, left)

    lines = []
    for mode in (0, 1):
        occ = 1.0 / (jnp.exp(freqs[mode]) - 1.0)
        lines.append((freqs[mode].T, jnp.sqrt(occ * (occ + 1.0)).T))
    for f in (0, 1):
        for q, value in enumerate(lines[f] + lines[1 - f]):
            rows[pl.ds(f * trip * 8 + q, trip, stride=8), 0:bands] = value
    third = 1.0 / (jnp.exp(freqs[2]) - 1.0) + 1.0
    eye = (
        lax.broadcasted_iota(jnp.int32, (trip, trip), 0)
        == lax.broadcasted_iota(jnp.int32, (trip, trip), 1)
    ).astype(jnp.bfloat16)

    for i in range(pieces):
        fetch(i).wait()

        @pl.loop(i * piece, (i + 1) * piece, unroll=4)
        def _(j):
            scaled = (here[0, j].astype(jnp.float32) * third).astype(jnp.bfloat16)
            turned[pl.ds(j, trip, stride=bands), 0:bands] = scaled.T.astype(jnp.float32)
            other = lax.dot_general(
                eye, here[1, j], (((1,), (1,)), ((), ())), preferred_element_type=jnp.float32
            )
            turned[pl.ds(trip * bands + j, trip, stride=bands), 0:bands] = other

    def send(t):
        e = place[t]
        return pltpu.make_async_copy(block.at[t], out.at[e], out_sem)

    @pl.loop(0, trip // group)
    def _(g):
        for u in range(group):
            t = g * group + u
            f = flip[t]
            factors = [
                turned[pl.ds(pl.multiple_of((h * trip + t) * bands, 8), bands), 0:bands].astype(
                    jnp.bfloat16
                )
                for h in (f, 1 - f)
            ]
            core = lax.dot_general(
                *factors, (((1,), (1,)), ((), ())), preferred_element_type=jnp.float32
            )
            line = rows[pl.ds(pl.multiple_of((f * trip + t) * 8, 8), 8), :]
            column = line.T[0:bands]
            diff = column[:, 0:1] - line[2:3, 0:bands]
            scale = column[:, 1:2] * line[3:4, 0:bands] * jnp.exp(-diff * diff / 0.5)
            value = jnp.pad(scale * core, ((0, 0), (0, LANES - bands)))
            block[t] = value.reshape(block.shape[1:]).astype(block.dtype)
        for u in range(group):
            t = g * group + u

            @pl.when(place[t] >= 0)
            def _():
                send(t).start()

    @pl.loop(0, trip)
    def _(t):
        @pl.when(place[t] >= 0)
        def _():
            send(t).wait()


def make_blocks(strength, freqs, owner, tile, live, grid, plan, cells):
    trip, n_factor, bands, _ = strength.shape
    devices = grid[0] * grid[1]
    by_lane = strength.transpose(1, 2, 3, 0)
    freqs = freqs.transpose(1, 2, 0)
    smem = pl.BlockSpec(memory_space=pltpu.SMEM)
    anywhere = pl.BlockSpec(memory_space=pl.ANY)
    part = (PARTS, bands // PARTS, LANES)
    pieces = 6
    return pl.pallas_call(
        functools.partial(blocks_kernel, grid, plan, 8),
        name="blocks",
        out_shape=[
            jax.ShapeDtypeStruct((cells, *part), jnp.bfloat16),
            jax.ShapeDtypeStruct((devices, LANES), jnp.int32),
        ],
        in_specs=[smem, smem, smem, anywhere, pl.BlockSpec(memory_space=pltpu.VMEM)],
        out_specs=[anywhere, smem],
        scratch_shapes=[
            pltpu.VMEM(by_lane.shape, by_lane.dtype),
            pltpu.VMEM((2 * trip * bands, LANES), jnp.float32),
            pltpu.VMEM((2 * trip * 8, LANES), jnp.float32),
            pltpu.VMEM((trip, *part), jnp.bfloat16),
            pltpu.SMEM((cells,), jnp.int32),
            pltpu.SMEM((trip,), jnp.int32),
            pltpu.SMEM((trip,), jnp.int32),
            pltpu.SMEM((trip,), jnp.int32),
            pltpu.SemaphoreType.DMA((pieces,)),
            pltpu.SemaphoreType.DMA,
        ],
        compiler_params=pltpu.CompilerParams(vmem_limit_bytes=VMEM_BYTES),
    )(owner, tile, live, by_lane, freqs)


def sum_kernel(labels, one, two, out, total):
    step = pl.program_id(0)
    here = one.shape[0]
    tiles = out.shape[0]

    @pl.when(step == 0)
    def _():
        @pl.loop(0, tiles, unroll=4)
        def _(k):
            total[k] = jnp.zeros(total.shape[1:], jnp.float32)

    @pl.loop(0, here, unroll=4)
    def _(s):
        for r, got in enumerate((one, two)):
            label = labels[step * here + s, r]
            total[jnp.where(label < 0, tiles, label)] += got[s].astype(jnp.float32)

    @pl.when(step == pl.num_programs(0) - 1)
    def _():
        @pl.loop(0, tiles, unroll=4)
        def _(k):
            out[k] = total[k].astype(out.dtype)


def sum_tiles(labels, one, two, tiles):
    devices, *part = one.shape
    here = 32
    spec = pl.BlockSpec((here, *part), lambda i: (i, 0, 0, 0))
    return pl.pallas_call(
        sum_kernel,
        name="sum_tiles",
        grid=(devices // here,),
        out_shape=jax.ShapeDtypeStruct((tiles, *part), jnp.bfloat16),
        in_specs=[pl.BlockSpec(memory_space=pltpu.SMEM), spec, spec],
        out_specs=pl.BlockSpec(memory_space=pltpu.VMEM),
        scratch_shapes=[pltpu.VMEM((tiles + 1, *part), jnp.float32)],
        compiler_params=pltpu.CompilerParams(vmem_limit_bytes=VMEM_BYTES),
    )(labels, one, two)


def symmetrize_kernel(n_grp, omega, partner, out):
    per, thirds, part, lanes = omega.shape
    bands = thirds * part
    for k in range(per):
        turned = partner[k].astype(jnp.float32).reshape(bands, lanes).T
        mine = omega[k].astype(jnp.float32).reshape(bands, lanes)
        i, c = divmod(k, n_grp)
        out[i, pl.ds(c, bands, stride=n_grp), :] = 0.5 * (mine[:, 0:bands] + turned[0:bands])


def symmetrize(omega, partner, n_grp):
    tiles, thirds, part, lanes = omega.shape
    bands = thirds * part
    rows = 8
    spec = pl.BlockSpec((rows * n_grp, thirds, part, lanes), lambda i: (i, 0, 0, 0))
    return pl.pallas_call(
        functools.partial(symmetrize_kernel, n_grp),
        name="symmetrize",
        grid=(tiles // (rows * n_grp),),
        out_shape=jax.ShapeDtypeStruct((tiles // n_grp, bands * n_grp, bands), jnp.float32),
        in_specs=[spec, spec],
        out_specs=pl.BlockSpec((rows, bands * n_grp, bands), lambda i: (i, 0, 0)),
        compiler_params=pltpu.CompilerParams(vmem_limit_bytes=VMEM_BYTES),
    )(omega, partner)


def per_device(strength, freqs, owner, tile_slot, live_count):
    bands = strength.shape[2]
    n_grp = lax.axis_size("grp")
    n_dev = lax.axis_size("dev")
    grid = (n_grp, n_dev)
    devices = n_grp * n_dev
    part = (PARTS, bands // PARTS, LANES)
    torus = (SIDE, SIDE, SIDE)
    plain = ((0, 1, 2, 3), (0, 1, 2, 3), False)
    args = (strength, freqs, owner[:, 0], tile_slot, live_count, grid)

    def with_labels(labels):
        return labels.reshape(*torus, 2, 1, 1, LANES)

    cells, labels = make_blocks(*args, plan_shared, devices * 3 // 2)
    own, labels, shared = exchange(
        [cells.reshape(3, *torus, *part), with_labels(labels)],
        [((1, 2, 3, 0), (0, 1, 2, 3), True), plain],
        1,
        "send_blocks",
    )
    labels = labels.reshape(devices, LANES)

    def sum_shared():
        return sum_tiles(
            labels, own.reshape(devices, *part), shared.reshape(devices, *part), devices
        )

    def sum_dense():
        cells, labels = make_blocks(*args, plan_dense, devices * 2)
        cells = cells.reshape(2, 2, *torus, *part)
        moved = ((1, 2, 3, 0), (0, 1, 2, 3), False)
        one, two, labels = exchange(
            [cells[0], cells[1], with_labels(labels)], [moved, moved, plain], 3, "send_dense"
        )
        return sum_tiles(
            labels.reshape(devices, LANES),
            one.reshape(devices, *part),
            two.reshape(devices, *part),
            devices,
        )

    omega = lax.cond(jnp.any(labels[:, 2] > 0), sum_dense, sum_shared)
    by_dev = ((3, 0, 1, 2), (3, 0, 1, 2), False)
    (partner,) = exchange(
        [omega.reshape(SIDE, SIDE, 2, n_grp, *part)], [by_dev], 2, "send_tiles"
    )
    sym = symmetrize(omega, partner.reshape(omega.shape), n_grp)
    return sym.reshape(devices // n_grp, bands, n_grp, 1, bands)


def solution(mesh):
    return jax.shard_map(
        per_device,
        mesh=mesh,
        in_specs=(
            P(("grp", "dev"), None, None, None),
            P(("grp", "dev"), None, None),
            P(("grp", "dev"), None),
            P(("grp", "dev")),
            P(("grp", "dev")),
        ),
        out_specs=P("grp", None, None, "dev", None),
        check_vma=False,
    )
```

```python
import functools

import jax
import jax.numpy as jnp
from jax import lax
from jax.experimental import pallas as pl
from jax.experimental.pallas import tpu as pltpu
from jax.sharding import PartitionSpec as P

MESH = pl.DeviceIdType.MESH
LANES = 128
SIDE = 4
VMEM_BYTES = 56 * 2**20


PARTS = 3
WALK = 400
PIECES = 6


def position():
    g, d = lax.axis_index("grp"), lax.axis_index("dev")
    return g, d // 8, lax.rem(d // 2, 4), lax.rem(d, 2)


def device_at(pos, axis, step, flip):
    at = list(pos)
    if step:
        at[axis] = lax.rem(pos[axis] + step, SIDE)
    if flip:
        at[3] = 1 - pos[3]
    return at[0], (at[1] * SIDE + at[2]) * 2 + at[3]


def exchange_kernel(plans, *refs):
    n = len(plans)
    srcs, dsts, firsts, seconds = (refs[k * n : (k + 1) * n] for k in range(4))
    send_sem, recv_sem, own_sem = refs[4 * n :]
    pos = position()
    steps = (1, 3, 2)

    barrier = pltpu.get_barrier_semaphore()
    greeted = [(a, r, f) for a in range(3) for r in (1, 2, 3) for f in (False, True)]
    greeted.append((0, 0, True))
    for a, r, f in greeted:
        pl.semaphore_signal(
            barrier, inc=1, device_id=device_at(pos, a, r, f), device_id_type=MESH
        )
    pl.semaphore_wait(barrier, len(greeted))

    def view(ref, places, front, p, axis, at, core):
        index = [slice(None)] * 4
        index[places[axis]] = at
        index[places[3]] = core
        return ref.at[(p,) + tuple(index)] if front else ref.at[tuple(index) + (p,)]

    def ends(stage, k, f, p, step):
        src_places, dst_places = plans[k]
        axis = (p + stage) % 3
        there = lax.rem(pos[axis] + step, SIDE) if step else pos[axis]
        core = (pos[3], 1 - pos[3])[f]
        source = view((srcs, firsts, seconds)[stage][k], src_places, stage > 0, p, axis, there, core)
        if stage < 2:
            target = view((firsts, seconds)[stage][k], src_places, True, p, axis, pos[axis], core)
        else:
            target = view(dsts[k], dst_places, False, p, axis, pos[axis], pos[3])
        return source, target

    def remote(stage, k, f, p, m):
        step = (*steps, 0)[m]
        source, target = ends(stage, k, f, p, step)
        return pltpu.make_async_remote_copy(
            src_ref=source,
            dst_ref=target,
            send_sem=send_sem.at[stage, k, f, p, m],
            recv_sem=recv_sem.at[stage, k, f, p, m],
            device_id=device_at(pos, (p + stage) % 3, step, stage == 2 and f == 1),
            device_id_type=MESH,
        )

    def copies(stage, k, f, p):
        if stage == 2 and f == 1:
            return [remote(stage, k, f, p, m) for m in range(4)], []
        source, target = ends(stage, k, f, p, 0)
        return (
            [remote(stage, k, f, p, m) for m in range(3)],
            [pltpu.make_async_copy(source, target, own_sem.at[stage, k, f, p])],
        )

    def start(*job):
        for group in copies(*job):
            for copy in group:
                copy.start()

    def arrive(*job):
        remotes, locals_ = copies(*job)
        for copy in remotes:
            copy.wait_recv()
        for copy in locals_:
            copy.wait()

    jobs = [
        (k, f, p)
        for f in (1, 0)
        for p in range(PARTS)
        for k in range(n)
        if p < firsts[k].shape[0]
    ]
    for job in jobs:
        start(0, *job)
    for stage in (1, 2):
        for job in jobs:
            arrive(stage - 1, *job)
            start(stage, *job)
    for job in jobs:
        arrive(2, *job)
    for stage in range(3):
        for job in jobs:
            for copy in copies(stage, *job)[0]:
                copy.wait_send()


def exchange(arrays, plans, collective_id, name):
    n = len(arrays)
    outs, temps = [], []
    for a, (src_places, dst_places) in zip(arrays, plans):
        front = [0] * 4
        for axis in range(4):
            front[dst_places[axis]] = a.shape[src_places[axis]]
        rest = a.shape[4:]
        outs.append(jax.ShapeDtypeStruct((*front, *rest), a.dtype))
        temps.append(pltpu.VMEM((rest[0],) + a.shape[:4] + rest[1:], a.dtype))
    anywhere = pl.BlockSpec(memory_space=pl.ANY)
    return pl.pallas_call(
        functools.partial(exchange_kernel, plans),
        name=name,
        out_shape=outs,
        in_specs=[anywhere] * n,
        out_specs=[anywhere] * n,
        scratch_shapes=temps
        + temps
        + [pltpu.SemaphoreType.DMA((3, n, 2, PARTS, 4))] * 2
        + [pltpu.SemaphoreType.DMA((3, n, 2, PARTS))],
        compiler_params=pltpu.CompilerParams(
            collective_id=collective_id, has_side_effects=True, vmem_limit_bytes=VMEM_BYTES
        ),
    )(*arrays)


def plan_kernel(grid, owner, tile, live, cell, turn, labels, left):
    n_grp, n_dev = grid
    devices = n_grp * n_dev
    chips = devices // 2

    @pl.loop(0, devices, unroll=8)
    def _(o):
        labels[o, 0] = -1
        labels[o, 1] = -1
        labels[o, 2] = 0

    @pl.loop(0, cell.shape[0], unroll=8)
    def _(e):
        cell[e] = -1
        turn[e] = 0

    def first(t, n):
        o = owner[t]
        e = lax.rem(o, 2) * chips + lax.div(o, 2)
        taken = cell[e] >= 0

        @pl.when(jnp.logical_not(taken))
        def _():
            cell[e] = t
            labels[o, 0] = tile[t]

        @pl.when(taken)
        def _():
            left[n] = t

        return n + taken.astype(jnp.int32)

    n_left = lax.fori_loop(0, live[0], first, jnp.int32(0))

    def insert(q, carry):
        lost, noise = carry

        def body(state):
            t, steps, noise = state
            o, k = owner[t], tile[t]
            x = lax.rem(k, n_grp) * n_dev + lax.div(k, n_grp)
            e0 = lax.rem(o, 2) * chips + lax.div(o, 2)
            e1 = devices + lax.div(o, 2)
            e2 = lax.rem(x, 2) * chips + lax.div(x, 2)
            e3 = devices + lax.div(x, 2)
            noise = lax.rem(noise * 1103 + 12345, 65521)
            pick = lax.rem(lax.div(noise, 8), 4)
            for r, e in ((3, e3), (2, e2), (0, e0), (1, e1)):
                pick = jnp.where(cell[e] < 0, r, pick)
            e = jnp.where(pick == 0, e0, jnp.where(pick == 1, e1, jnp.where(pick == 2, e2, e3)))
            turned = pick >= 2
            to = jnp.where(turned, x, o)
            label = jnp.where(turned, lax.rem(o, n_dev) * n_grp + lax.div(o, n_dev), k)
            victim = cell[e]
            cell[e] = t
            turn[e] = turned.astype(jnp.int32)
            both = (e >= devices).astype(jnp.int32)
            labels[to, both] = label

            @pl.when(e >= devices)
            def _():
                labels[to + 1 - 2 * lax.rem(to, 2), 1] = -1

            return victim, steps + 1, noise

        t, _, noise = lax.while_loop(
            lambda state: (state[0] >= 0) & (state[1] < WALK), body, (left[q], 0, noise)
        )
        return lost | (t >= 0).astype(jnp.int32), noise

    lost, _ = lax.fori_loop(0, n_left, insert, (jnp.int32(0), jnp.int32(1)))

    @pl.when(lost > 0)
    def _():
        @pl.loop(0, devices)
        def _(o):
            labels[o, 2] = 1


def make_plan(owner, tile, live, grid):
    devices = grid[0] * grid[1]
    smem = pl.BlockSpec(memory_space=pltpu.SMEM)
    cells = jax.ShapeDtypeStruct((devices * 3 // 2,), jnp.int32)
    return pl.pallas_call(
        functools.partial(plan_kernel, grid),
        name="plan",
        out_shape=[cells, cells, jax.ShapeDtypeStruct((devices, LANES), jnp.int32)],
        in_specs=[smem] * 3,
        out_specs=[smem] * 3,
        scratch_shapes=[pltpu.SMEM(tile.shape, jnp.int32)],
    )(owner, tile, live)


def fetch_copies(strength, here, in_sem):
    pieces = in_sem.shape[0]
    piece = strength.shape[1] // pieces
    return [
        pltpu.make_async_copy(
            strength.at[:, pl.ds(i * piece, piece)],
            here.at[:, pl.ds(i * piece, piece)],
            in_sem.at[i],
        )
        for i in range(pieces)
    ]


def turn_factors(fetches, freqs, here, turned, rows):
    _, bands, _, trip = here.shape
    flat = turned.reshape(2 * trip * bands, LANES)
    flat_rows = rows.reshape(2 * trip * 8, LANES)
    lines = []
    for mode in (0, 1):
        occ = 1.0 / (jnp.exp(freqs[mode]) - 1.0)
        lines.append((freqs[mode].T, jnp.sqrt(occ * (occ + 1.0)).T))
    for f in (0, 1):
        for q, value in enumerate(lines[f] + lines[1 - f]):
            flat_rows[pl.ds(f * trip * 8 + q, trip, stride=8), 0:bands] = value
    third = 1.0 / (jnp.exp(freqs[2]) - 1.0) + 1.0
    eye = (
        lax.broadcasted_iota(jnp.int32, (trip, trip), 0)
        == lax.broadcasted_iota(jnp.int32, (trip, trip), 1)
    ).astype(jnp.bfloat16)
    piece = bands // len(fetches)
    for i, fetch in enumerate(fetches):
        fetch.wait()

        @pl.loop(i * piece, (i + 1) * piece, unroll=10)
        def _(j):
            scaled = (here[0, j].astype(jnp.float32) * third).astype(jnp.bfloat16)
            flat[pl.ds(j, trip, stride=bands), 0:bands] = scaled.T.astype(jnp.float32)
            other = lax.dot_general(
                eye, here[1, j], (((1,), (1,)), ((), ())), preferred_element_type=jnp.float32
            )
            flat[pl.ds(trip * bands + j, trip, stride=bands), 0:bands] = other


def block_of(turned, rows, trip, bands, t, f):
    factors = [
        turned[h * trip + t][:, 0:bands].astype(jnp.bfloat16) for h in (f, 1 - f)
    ]
    core = lax.dot_general(
        *factors, (((1,), (1,)), ((), ())), preferred_element_type=jnp.float32
    )
    line = rows[f * trip + t]
    column = line.T[0:bands]
    diff = column[:, 0:1] - line[2:3, 0:bands]
    scale = column[:, 1:2] * line[3:4, 0:bands] * jnp.exp(-diff * diff / 0.5)
    value = jnp.pad(scale * core, ((0, 0), (0, LANES - bands)))
    return value.reshape(PARTS, bands // PARTS, LANES).astype(jnp.bfloat16)


def dense_kernel(
    grid, owner, tile, live, strength, freqs, out, labels,
    here, turned, rows, block, cell, place, in_sem, out_sem,
):
    _, bands, _, trip = strength.shape
    devices = grid[0] * grid[1]
    chips = devices // 2
    fetches = fetch_copies(strength, here, in_sem)
    for fetch in fetches:
        fetch.start()

    @pl.loop(0, devices)
    def _(o):
        labels[o, 0] = -1
        labels[o, 1] = -1
        cell[o] = 0

    @pl.loop(0, trip)
    def _(t):
        place[t] = -1

    @pl.loop(0, live[0])
    def _(t):
        o = owner[t]
        r = cell[o]
        cell[o] = r + 1
        place[t] = (r * 2 + lax.rem(o, 2)) * chips + lax.div(o, 2)
        labels[o, r] = tile[t]

    turn_factors(fetches, freqs, here, turned, rows)

    def send(t):
        return pltpu.make_async_copy(block.at[t], out.at[place[t]], out_sem)

    @pl.loop(0, trip)
    def _(t):
        block[t] = block_of(turned, rows, trip, bands, t, 0)

        @pl.when(place[t] >= 0)
        def _():
            send(t).start()

    @pl.loop(0, trip)
    def _(t):
        @pl.when(place[t] >= 0)
        def _():
            send(t).wait()


def dense_blocks(strength, freqs, owner, tile, live, grid):
    _, bands, _, trip = strength.shape
    devices = grid[0] * grid[1]
    smem = pl.BlockSpec(memory_space=pltpu.SMEM)
    anywhere = pl.BlockSpec(memory_space=pl.ANY)
    part = (PARTS, bands // PARTS, LANES)
    return pl.pallas_call(
        functools.partial(dense_kernel, grid),
        name="dense_blocks",
        out_shape=[
            jax.ShapeDtypeStruct((devices * 2, *part), jnp.bfloat16),
            jax.ShapeDtypeStruct((devices, LANES), jnp.int32),
        ],
        in_specs=[smem, smem, smem, anywhere, pl.BlockSpec(memory_space=pltpu.VMEM)],
        out_specs=[anywhere, smem],
        scratch_shapes=[
            pltpu.VMEM(strength.shape, strength.dtype),
            pltpu.VMEM((2 * trip, bands, LANES), jnp.float32),
            pltpu.VMEM((2 * trip, 8, LANES), jnp.float32),
            pltpu.VMEM((trip, *part), jnp.bfloat16),
            pltpu.SMEM((devices,), jnp.int32),
            pltpu.SMEM((trip,), jnp.int32),
            pltpu.SemaphoreType.DMA((PIECES,)),
            pltpu.SemaphoreType.DMA,
        ],
        compiler_params=pltpu.CompilerParams(vmem_limit_bytes=VMEM_BYTES),
    )(owner, tile, live, strength, freqs)


def send_blocks_kernel(
    cell, turn, strength, freqs, labels, own_out, labels_out, shared_out,
    here, turned, rows, staged, first, second, shared_in, labels_first, labels_second,
    in_sem, send_sem, recv_sem, own_sem, last_send, last_recv, last_own, labels_send, labels_recv, labels_own,
):
    _, bands, _, trip = strength.shape
    pos = position()
    steps = (1, 3, 2)
    slabs = (1, 3, 2, 0)
    fetches = fetch_copies(strength, here, in_sem)
    for fetch in fetches:
        fetch.start()

    barrier = pltpu.get_barrier_semaphore()
    greeted = [(a, r, f) for a in range(3) for r in (1, 2, 3) for f in (False, True)]
    greeted.append((0, 0, True))
    for a, r, f in greeted:
        pl.semaphore_signal(
            barrier, inc=1, device_id=device_at(pos, a, r, f), device_id_type=MESH
        )
    turn_factors(fetches, freqs, here, turned, rows)
    pl.semaphore_wait(barrier, len(greeted))

    def moved(axis, step):
        return lax.rem(pos[axis] + step, SIDE) if step else pos[axis]

    def compute(x):
        @pl.loop(0, 6)
        def _(i):
            k, half = lax.div(i, 2), lax.rem(i, 2)
            for u in range(8):
                e = k * SIDE**3 + x * SIDE**2 + half * 8 + u
                t = jnp.maximum(cell[e], 0)
                staged[k, x, half * 2 + u // SIDE, u % SIDE] = block_of(
                    turned, rows, trip, bands, t, turn[e]
                )

    def cut(ref, front, p, core, **at):
        index = [core] + [at.get(name, slice(None)) for name in "xyz"]
        return ref.at[(p, *index)] if front else ref.at[(*index, p)]

    def early(stage, p, q):
        axis = (p + stage) % 3
        source, target = ((staged, first), (first, second))[stage]

        def ends(step):
            if axis == 0:
                there, here_at = {"x": moved(0, step)}, {"x": pos[0]}
            else:
                r = slabs[q]
                x = moved(0, (SIDE - r) % SIDE if p == 0 else r)
                there = {"x": x, "xyz"[axis]: moved(axis, step)}
                here_at = {"x": x, "xyz"[axis]: pos[axis]}
            return (
                cut(source, stage > 0, p, slice(None), **there),
                cut(target, True, p, slice(None), **here_at),
            )

        def remote(m, step):
            source_at, target_at = ends(step)
            return pltpu.make_async_remote_copy(
                src_ref=source_at,
                dst_ref=target_at,
                send_sem=send_sem.at[stage, p, q, m],
                recv_sem=recv_sem.at[stage, p, q, m],
                device_id=device_at(pos, axis, step, False),
                device_id_type=MESH,
            )

        def local():
            return pltpu.make_async_copy(*ends(0), own_sem.at[stage, p, q])

        if axis == 0:
            return ([remote(0, slabs[q])], []) if slabs[q] else ([], [local()])
        return [remote(m, step) for m, step in enumerate(steps)], [local()]

    def late(p, f, m):
        axis = (p + 2) % 3
        step = (*steps, 0)[m]
        core = (pos[3], 1 - pos[3], 2)[f]
        there, here_at = {"xyz"[axis]: moved(axis, step)}, {"xyz"[axis]: pos[axis]}
        source = cut(second, True, p, core, **there)
        index = [here_at.get(name, slice(None)) for name in "xyz"]
        if f < 2:
            target = own_out.at[(*index, pos[3], p)]
        else:
            target = shared_in.at[(p, *index)]
        if step == 0 and f != 1:
            return pltpu.make_async_copy(source, target, last_own.at[p, f])
        return pltpu.make_async_remote_copy(
            src_ref=source,
            dst_ref=target,
            send_sem=last_send.at[p, f, m],
            recv_sem=last_recv.at[p, f, m],
            device_id=device_at(pos, axis, step, f == 1),
            device_id_type=MESH,
        )

    def is_local(f, m):
        return m == 3 and f != 1

    def pass_on(p):
        target = shared_out.at[:, :, :, pos[3], p]
        there = pltpu.make_async_remote_copy(
            src_ref=shared_in.at[p],
            dst_ref=target,
            send_sem=last_send.at[p, 3, 0],
            recv_sem=last_recv.at[p, 3, 0],
            device_id=device_at(pos, 0, 0, True),
            device_id_type=MESH,
        )
        return there, pltpu.make_async_copy(shared_in.at[p], target, last_own.at[p, 1])

    def label_messages(stage):
        source, target = (
            (labels, labels_first), (labels_first, labels_second), (labels_second, labels_out)
        )[stage]
        moves = [(r, f) for r in steps for f in (False, True)[: 1 + stage // 2]]
        moves += [(0, True)] if stage == 2 else []

        def ends(step, flip):
            at = [slice(None)] * 4
            to = [slice(None)] * 4
            at[stage], to[stage] = moved(stage, step), pos[stage]
            if stage == 2:
                at[3], to[3] = 1 - pos[3] if flip else pos[3], pos[3]
            return source.at[tuple(at)], target.at[tuple(to)]

        remotes = []
        for m, (step, flip) in enumerate(moves):
            source_at, target_at = ends(step, flip)
            remotes.append(
                pltpu.make_async_remote_copy(
                    src_ref=source_at,
                    dst_ref=target_at,
                    send_sem=labels_send.at[stage, m],
                    recv_sem=labels_recv.at[stage, m],
                    device_id=device_at(pos, stage, step, flip),
                    device_id_type=MESH,
                )
            )
        return remotes, [pltpu.make_async_copy(*ends(0, False), labels_own.at[stage])]

    def start(messages):
        for group in messages:
            for copy in group:
                copy.start()

    def arrive(messages):
        remotes, locals_ = messages
        for copy in remotes:
            copy.wait_recv()
        for copy in locals_:
            copy.wait()

    start(label_messages(0))
    for q in range(SIDE):
        compute(moved(0, slabs[q]))
        for p in range(PARTS):
            start(early(0, p, q))
    arrive(label_messages(0))
    start(label_messages(1))
    for q in range(SIDE):
        for p in range(PARTS):
            arrive(early(0, p, q))
            start(early(1, p, q))
    arrive(label_messages(1))
    start(label_messages(2))
    for q in range(SIDE):
        arrive(early(1, 1, q))
        m = (*steps, 0).index(slabs[q])
        for f in (2, 1, 0):
            late(1, f, m).start()
    for p in (0, 2):
        for q in range(SIDE):
            arrive(early(1, p, q))
        for f in (2, 1, 0):
            for m in range(4):
                late(p, f, m).start()
    arrive(label_messages(2))
    for f in (2, 1, 0):
        for p in (1, 0, 2):
            for m in range(4):
                if is_local(f, m):
                    late(p, f, m).wait()
                else:
                    late(p, f, m).wait_recv()
            if f == 2:
                for copy in pass_on(p):
                    copy.start()
    for p in range(PARTS):
        there, at_home = pass_on(p)
        there.wait()
        at_home.wait()
        for f in range(3):
            for m in range(4):
                if not is_local(f, m):
                    late(p, f, m).wait_send()
        for stage in range(2):
            for q in range(SIDE):
                for copy in early(stage, p, q)[0]:
                    copy.wait_send()
    for stage in range(3):
        for copy in label_messages(stage)[0]:
            copy.wait_send()


def send_blocks(cell, turn, labels, strength, freqs, collective_id):
    _, bands, _, trip = strength.shape
    part = (bands // PARTS, LANES)
    torus = (SIDE, SIDE, SIDE)
    moving = pltpu.VMEM((PARTS, 3, *torus, *part), jnp.bfloat16)
    arrived = jax.ShapeDtypeStruct((*torus, 2, PARTS, *part), jnp.bfloat16)
    smem = pl.BlockSpec(memory_space=pltpu.SMEM)
    anywhere = pl.BlockSpec(memory_space=pl.ANY)
    dma = pltpu.SemaphoreType.DMA
    return pl.pallas_call(
        send_blocks_kernel,
        name="send_blocks",
        out_shape=[arrived, jax.ShapeDtypeStruct(labels.shape, labels.dtype), arrived],
        in_specs=[smem, smem, anywhere, pl.BlockSpec(memory_space=pltpu.VMEM), anywhere],
        out_specs=[anywhere] * 3,
        scratch_shapes=[
            pltpu.VMEM(strength.shape, strength.dtype),
            pltpu.VMEM((2 * trip, bands, LANES), jnp.float32),
            pltpu.VMEM((2 * trip, 8, LANES), jnp.float32),
            pltpu.VMEM((3, *torus, PARTS, *part), jnp.bfloat16),
            moving,
            moving,
            pltpu.VMEM((PARTS, *torus, *part), jnp.bfloat16),
            pltpu.VMEM(labels.shape, labels.dtype),
            pltpu.VMEM(labels.shape, labels.dtype),
            dma((PIECES,)),
            dma((2, PARTS, SIDE, 3)),
            dma((2, PARTS, SIDE, 3)),
            dma((2, PARTS, SIDE)),
            dma((PARTS, 4, 4)),
            dma((PARTS, 4, 4)),
            dma((PARTS, 3)),
            dma((3, 7)),
            dma((3, 7)),
            dma((3,)),
        ],
        compiler_params=pltpu.CompilerParams(
            collective_id=collective_id, has_side_effects=True, vmem_limit_bytes=VMEM_BYTES
        ),
    )(cell, turn, strength, freqs, labels)


def sum_kernel(labels, one, two, out, total):
    step = pl.program_id(0)
    here = one.shape[0]
    tiles = out.shape[0]

    @pl.when(step == 0)
    def _():
        @pl.loop(0, tiles, unroll=4)
        def _(k):
            total[k] = jnp.zeros(total.shape[1:], jnp.float32)

    @pl.loop(0, here, unroll=4)
    def _(s):
        for r, got in enumerate((one, two)):
            label = labels[step * here + s, r]
            total[jnp.where(label < 0, tiles, label)] += got[s].astype(jnp.float32)

    @pl.when(step == pl.num_programs(0) - 1)
    def _():
        @pl.loop(0, tiles, unroll=4)
        def _(k):
            out[k] = total[k].astype(out.dtype)


def sum_tiles(labels, one, two, tiles):
    devices, *part = one.shape
    here = 32
    spec = pl.BlockSpec((here, *part), lambda i: (i, 0, 0, 0))
    return pl.pallas_call(
        sum_kernel,
        name="sum_tiles",
        grid=(devices // here,),
        out_shape=jax.ShapeDtypeStruct((tiles, *part), jnp.bfloat16),
        in_specs=[pl.BlockSpec(memory_space=pltpu.SMEM), spec, spec],
        out_specs=pl.BlockSpec(memory_space=pltpu.VMEM),
        scratch_shapes=[pltpu.VMEM((tiles + 1, *part), jnp.float32)],
        compiler_params=pltpu.CompilerParams(vmem_limit_bytes=VMEM_BYTES),
    )(labels, one, two)


def symmetrize_kernel(n_grp, omega, partner, out):
    per, thirds, part, lanes = omega.shape
    bands = thirds * part
    for k in range(per):
        turned = partner[k].astype(jnp.float32).reshape(bands, lanes).T
        mine = omega[k].astype(jnp.float32).reshape(bands, lanes)
        i, c = divmod(k, n_grp)
        out[i, pl.ds(c, bands, stride=n_grp), :] = 0.5 * (mine[:, 0:bands] + turned[0:bands])


def symmetrize(omega, partner, n_grp):
    tiles, thirds, part, lanes = omega.shape
    bands = thirds * part
    rows = 8
    spec = pl.BlockSpec((rows * n_grp, thirds, part, lanes), lambda i: (i, 0, 0, 0))
    return pl.pallas_call(
        functools.partial(symmetrize_kernel, n_grp),
        name="symmetrize",
        grid=(tiles // (rows * n_grp),),
        out_shape=jax.ShapeDtypeStruct((tiles // n_grp, bands * n_grp, bands), jnp.float32),
        in_specs=[spec, spec],
        out_specs=pl.BlockSpec((rows, bands * n_grp, bands), lambda i: (i, 0, 0)),
        compiler_params=pltpu.CompilerParams(vmem_limit_bytes=VMEM_BYTES),
    )(omega, partner)


def per_device(strength, freqs, owner, tile_slot, live_count):
    bands = strength.shape[2]
    n_grp = lax.axis_size("grp")
    n_dev = lax.axis_size("dev")
    grid = (n_grp, n_dev)
    devices = n_grp * n_dev
    part = (PARTS, bands // PARTS, LANES)
    torus = (SIDE, SIDE, SIDE)
    plain = ((0, 1, 2, 3), (0, 1, 2, 3))
    by_lane, freqs = strength.transpose(1, 2, 3, 0), freqs.transpose(1, 2, 0)
    names = (owner[:, 0], tile_slot, live_count)

    def with_labels(labels):
        return labels.reshape(*torus, 2, 1, 1, LANES)

    cell, turn, labels = make_plan(*names, grid)
    own, labels, shared = send_blocks(cell, turn, with_labels(labels), by_lane, freqs, 1)
    labels = labels.reshape(devices, LANES)

    def sum_shared():
        return sum_tiles(
            labels, own.reshape(devices, *part), shared.reshape(devices, *part), devices
        )

    def sum_dense():
        cells, labels = dense_blocks(by_lane, freqs, *names, grid)
        cells = cells.reshape(2, 2, *torus, *part)
        moved = ((1, 2, 3, 0), (0, 1, 2, 3))
        one, two, labels = exchange(
            [cells[0], cells[1], with_labels(labels)], [moved, moved, plain], 3, "send_dense"
        )
        return sum_tiles(
            labels.reshape(devices, LANES),
            one.reshape(devices, *part),
            two.reshape(devices, *part),
            devices,
        )

    omega = lax.cond(jnp.any(labels[:, 2] > 0), sum_dense, sum_shared)
    by_dev = ((3, 0, 1, 2), (3, 0, 1, 2))
    (partner,) = exchange(
        [omega.reshape(SIDE, SIDE, 2, n_grp, *part)], [by_dev], 2, "send_tiles"
    )
    sym = symmetrize(omega, partner.reshape(omega.shape), n_grp)
    return sym.reshape(devices // n_grp, bands, n_grp, 1, bands)


def solution(mesh):
    return jax.shard_map(
        per_device,
        mesh=mesh,
        in_specs=(
            P(("grp", "dev"), None, None, None),
            P(("grp", "dev"), None, None),
            P(("grp", "dev"), None),
            P(("grp", "dev")),
            P(("grp", "dev")),
        ),
        out_specs=P("grp", None, None, "dev", None),
        check_vma=False,
    )
```

```python
import functools

import jax
import jax.numpy as jnp
from jax import lax
from jax.experimental import pallas as pl
from jax.experimental.pallas import tpu as pltpu
from jax.sharding import PartitionSpec as P

MESH = pl.DeviceIdType.MESH
LANES = 128
SIDE = 4
VMEM_BYTES = 56 * 2**20


PARTS = 3
WALK = 400
PIECES = 12


def position():
    g, d = lax.axis_index("grp"), lax.axis_index("dev")
    return g, d // 8, lax.rem(d // 2, 4), lax.rem(d, 2)


def device_at(pos, axis, step, flip):
    at = list(pos)
    if step:
        at[axis] = lax.rem(pos[axis] + step, SIDE)
    if flip:
        at[3] = 1 - pos[3]
    return at[0], (at[1] * SIDE + at[2]) * 2 + at[3]


def exchange_kernel(plans, *refs):
    n = len(plans)
    srcs, dsts, firsts, seconds = (refs[k * n : (k + 1) * n] for k in range(4))
    send_sem, recv_sem, own_sem = refs[4 * n :]
    pos = position()
    steps = (1, 3, 2)

    barrier = pltpu.get_barrier_semaphore()
    greeted = [(a, r, f) for a in range(3) for r in (1, 2, 3) for f in (False, True)]
    greeted.append((0, 0, True))
    for a, r, f in greeted:
        pl.semaphore_signal(
            barrier, inc=1, device_id=device_at(pos, a, r, f), device_id_type=MESH
        )
    pl.semaphore_wait(barrier, len(greeted))

    def view(ref, places, front, p, axis, at, core):
        index = [slice(None)] * 4
        index[places[axis]] = at
        index[places[3]] = core
        return ref.at[(p,) + tuple(index)] if front else ref.at[tuple(index) + (p,)]

    def ends(stage, k, f, p, step):
        src_places, dst_places = plans[k]
        axis = (p + stage) % 3
        there = lax.rem(pos[axis] + step, SIDE) if step else pos[axis]
        core = (pos[3], 1 - pos[3])[f]
        source = view((srcs, firsts, seconds)[stage][k], src_places, stage > 0, p, axis, there, core)
        if stage < 2:
            target = view((firsts, seconds)[stage][k], src_places, True, p, axis, pos[axis], core)
        else:
            target = view(dsts[k], dst_places, False, p, axis, pos[axis], pos[3])
        return source, target

    def remote(stage, k, f, p, m):
        step = (*steps, 0)[m]
        source, target = ends(stage, k, f, p, step)
        return pltpu.make_async_remote_copy(
            src_ref=source,
            dst_ref=target,
            send_sem=send_sem.at[stage, k, f, p, m],
            recv_sem=recv_sem.at[stage, k, f, p, m],
            device_id=device_at(pos, (p + stage) % 3, step, stage == 2 and f == 1),
            device_id_type=MESH,
        )

    def copies(stage, k, f, p):
        if stage == 2 and f == 1:
            return [remote(stage, k, f, p, m) for m in range(4)], []
        source, target = ends(stage, k, f, p, 0)
        return (
            [remote(stage, k, f, p, m) for m in range(3)],
            [pltpu.make_async_copy(source, target, own_sem.at[stage, k, f, p])],
        )

    def start(*job):
        for group in copies(*job):
            for copy in group:
                copy.start()

    def arrive(*job):
        remotes, locals_ = copies(*job)
        for copy in remotes:
            copy.wait_recv()
        for copy in locals_:
            copy.wait()

    jobs = [
        (k, f, p)
        for f in (1, 0)
        for p in range(PARTS)
        for k in range(n)
        if p < firsts[k].shape[0]
    ]
    for job in jobs:
        start(0, *job)
    for stage in (1, 2):
        for job in jobs:
            arrive(stage - 1, *job)
            start(stage, *job)
    for job in jobs:
        arrive(2, *job)
    for stage in range(3):
        for job in jobs:
            for copy in copies(stage, *job)[0]:
                copy.wait_send()


def exchange(arrays, plans, collective_id, name):
    n = len(arrays)
    outs, temps = [], []
    for a, (src_places, dst_places) in zip(arrays, plans):
        front = [0] * 4
        for axis in range(4):
            front[dst_places[axis]] = a.shape[src_places[axis]]
        rest = a.shape[4:]
        outs.append(jax.ShapeDtypeStruct((*front, *rest), a.dtype))
        temps.append(pltpu.VMEM((rest[0],) + a.shape[:4] + rest[1:], a.dtype))
    anywhere = pl.BlockSpec(memory_space=pl.ANY)
    return pl.pallas_call(
        functools.partial(exchange_kernel, plans),
        name=name,
        out_shape=outs,
        in_specs=[anywhere] * n,
        out_specs=[anywhere] * n,
        scratch_shapes=temps
        + temps
        + [pltpu.SemaphoreType.DMA((3, n, 2, PARTS, 4))] * 2
        + [pltpu.SemaphoreType.DMA((3, n, 2, PARTS))],
        compiler_params=pltpu.CompilerParams(
            collective_id=collective_id, has_side_effects=True, vmem_limit_bytes=VMEM_BYTES
        ),
    )(*arrays)


def plan_kernel(grid, owner, tile, live, cell, turn, labels, left):
    n_grp, n_dev = grid
    devices = n_grp * n_dev
    chips = devices // 2

    @pl.loop(0, devices, unroll=8)
    def _(o):
        labels[0, o] = -1
        labels[1, o] = -1

    @pl.loop(0, cell.shape[0], unroll=8)
    def _(e):
        cell[e] = -1
        turn[e] = 0

    def first(t, n):
        o = owner[t]
        e = lax.rem(o, 2) * chips + lax.div(o, 2)
        held = cell[e]
        taken = held >= 0
        cell[e] = jnp.where(taken, held, t)
        labels[0, o] = jnp.where(taken, labels[0, o], tile[t])
        left[n] = t
        return n + taken.astype(jnp.int32)

    n_left = lax.fori_loop(0, live[0], first, jnp.int32(0))

    def insert(q, carry):
        lost, noise = carry

        def body(state):
            t, steps, noise = state
            o, k = owner[t], tile[t]
            x = lax.rem(k, n_grp) * n_dev + lax.div(k, n_grp)
            e0 = lax.rem(o, 2) * chips + lax.div(o, 2)
            e1 = devices + lax.div(o, 2)
            e2 = lax.rem(x, 2) * chips + lax.div(x, 2)
            e3 = devices + lax.div(x, 2)
            noise = lax.rem(noise * 1103 + 12345, 65521)
            pick = lax.rem(lax.div(noise, 8), 4)
            for r, e in ((3, e3), (2, e2), (0, e0), (1, e1)):
                pick = jnp.where(cell[e] < 0, r, pick)
            e = jnp.where(pick == 0, e0, jnp.where(pick == 1, e1, jnp.where(pick == 2, e2, e3)))
            turned = pick >= 2
            to = jnp.where(turned, x, o)
            label = jnp.where(turned, lax.rem(o, n_dev) * n_grp + lax.div(o, n_dev), k)
            victim = cell[e]
            cell[e] = t
            turn[e] = turned.astype(jnp.int32)
            both = (e >= devices).astype(jnp.int32)
            labels[both, to] = label

            @pl.when(e >= devices)
            def _():
                labels[1, to + 1 - 2 * lax.rem(to, 2)] = -1

            return victim, steps + 1, noise

        t, _, noise = lax.while_loop(
            lambda state: (state[0] >= 0) & (state[1] < WALK), body, (left[q], 0, noise)
        )
        return lost | (t >= 0).astype(jnp.int32), noise

    lost, _ = lax.fori_loop(0, n_left, insert, (jnp.int32(0), jnp.int32(1)))

    labels[2, 0] = lost


def make_plan(owner, tile, live, grid):
    devices = grid[0] * grid[1]
    smem = pl.BlockSpec(memory_space=pltpu.SMEM)
    cells = jax.ShapeDtypeStruct((devices * 3 // 2,), jnp.int32)
    return pl.pallas_call(
        functools.partial(plan_kernel, grid),
        name="plan",
        out_shape=[cells, cells, jax.ShapeDtypeStruct((3, devices), jnp.int32)],
        in_specs=[smem] * 3,
        out_specs=[smem] * 3,
        scratch_shapes=[pltpu.SMEM((tile.shape[0] + 1,), jnp.int32)],
    )(owner, tile, live)


def fetch_copies(strength, here, in_sem):
    pieces = in_sem.shape[0]
    piece = strength.shape[1] // pieces
    return [
        pltpu.make_async_copy(
            strength.at[:, pl.ds(i * piece, piece)],
            here.at[:, pl.ds(i * piece, piece)],
            in_sem.at[i],
        )
        for i in range(pieces)
    ]


def turn_factors(fetches, freqs, here, turned, rows):
    _, bands, _, trip = here.shape
    flat = turned.reshape(turned.shape[0] * bands, LANES)
    flat_rows = rows.reshape(2 * trip * 8, LANES)
    lines = []
    for mode in (0, 1):
        occ = 1.0 / (jnp.exp(freqs[mode]) - 1.0)
        lines.append((freqs[mode].T, jnp.sqrt(occ * (occ + 1.0)).T))
    for f in (0, 1):
        for q, value in enumerate(lines[f] + lines[1 - f]):
            flat_rows[pl.ds(f * trip * 8 + q, trip, stride=8), 0:bands] = value
    third = 1.0 / (jnp.exp(freqs[2]) - 1.0) + 1.0
    eye = (
        lax.broadcasted_iota(jnp.int32, (trip, trip), 0)
        == lax.broadcasted_iota(jnp.int32, (trip, trip), 1)
    ).astype(jnp.bfloat16)
    piece = bands // len(fetches)
    for i, fetch in enumerate(fetches):
        fetch.wait()

        @pl.loop(i * piece, (i + 1) * piece, unroll=10)
        def _(j):
            scaled = (here[0, j].astype(jnp.float32) * third).astype(jnp.bfloat16)
            flat[pl.ds(j, trip, stride=bands), 0:bands] = scaled.T.astype(jnp.float32)
            other = lax.dot_general(
                eye, here[1, j], (((1,), (1,)), ((), ())), preferred_element_type=jnp.float32
            )
            flat[pl.ds(trip * bands + j, trip, stride=bands), 0:bands] = other


def block_of(turned, rows, trip, bands, t, f):
    factors = [
        turned[h * trip + t][:, 0:bands].astype(jnp.bfloat16) for h in (f, 1 - f)
    ]
    core = lax.dot_general(
        *factors, (((1,), (1,)), ((), ())), preferred_element_type=jnp.float32
    )
    line = rows[f * trip + t]
    column = line.T[0:bands]
    diff = column[:, 0:1] - line[2:3, 0:bands]
    scale = column[:, 1:2] * line[3:4, 0:bands] * jnp.exp(-diff * diff / 0.5)
    value = jnp.pad(scale * core, ((0, 0), (0, LANES - bands)))
    return value.reshape(PARTS, bands // PARTS, LANES).astype(jnp.bfloat16)


def dense_kernel(
    grid, owner, tile, live, strength, freqs, out, labels,
    here, turned, rows, block, cell, place, in_sem, out_sem,
):
    _, bands, _, trip = strength.shape
    devices = grid[0] * grid[1]
    chips = devices // 2
    fetches = fetch_copies(strength, here, in_sem)
    for fetch in fetches:
        fetch.start()

    @pl.loop(0, devices)
    def _(o):
        labels[o, 0] = -1
        labels[o, 1] = -1
        cell[o] = 0

    @pl.loop(0, trip)
    def _(t):
        place[t] = -1

    @pl.loop(0, live[0])
    def _(t):
        o = owner[t]
        r = cell[o]
        cell[o] = r + 1
        place[t] = (r * 2 + lax.rem(o, 2)) * chips + lax.div(o, 2)
        labels[o, r] = tile[t]

    turn_factors(fetches, freqs, here, turned, rows)

    def send(t):
        return pltpu.make_async_copy(block.at[t], out.at[place[t]], out_sem)

    @pl.loop(0, trip)
    def _(t):
        block[t] = block_of(turned, rows, trip, bands, t, 0)

        @pl.when(place[t] >= 0)
        def _():
            send(t).start()

    @pl.loop(0, trip)
    def _(t):
        @pl.when(place[t] >= 0)
        def _():
            send(t).wait()


def dense_blocks(strength, freqs, owner, tile, live, grid):
    _, bands, _, trip = strength.shape
    devices = grid[0] * grid[1]
    smem = pl.BlockSpec(memory_space=pltpu.SMEM)
    anywhere = pl.BlockSpec(memory_space=pl.ANY)
    part = (PARTS, bands // PARTS, LANES)
    return pl.pallas_call(
        functools.partial(dense_kernel, grid),
        name="dense_blocks",
        out_shape=[
            jax.ShapeDtypeStruct((devices * 2, *part), jnp.bfloat16),
            jax.ShapeDtypeStruct((devices, LANES), jnp.int32),
        ],
        in_specs=[smem, smem, smem, anywhere, pl.BlockSpec(memory_space=pltpu.VMEM)],
        out_specs=[anywhere, smem],
        scratch_shapes=[
            pltpu.VMEM(strength.shape, strength.dtype),
            pltpu.VMEM((2 * trip, bands, LANES), jnp.float32),
            pltpu.VMEM((2 * trip, 8, LANES), jnp.float32),
            pltpu.VMEM((trip, *part), jnp.bfloat16),
            pltpu.SMEM((devices,), jnp.int32),
            pltpu.SMEM((trip,), jnp.int32),
            pltpu.SemaphoreType.DMA((PIECES,)),
            pltpu.SemaphoreType.DMA,
        ],
        compiler_params=pltpu.CompilerParams(vmem_limit_bytes=VMEM_BYTES),
    )(owner, tile, live, strength, freqs)


def main_kernel(
    cell, turn, names, strength, freqs, omega_out, partner_out, flag,
    here, turned, rows, staged, first, second, got_same, got_other, got_shared, tile_first, tile_second,
    labels, labels_first, labels_second, labels_third, known, table, listed,
    in_sem, send_sem, recv_sem, own_sem, last_send, last_recv, last_own, labels_send, labels_recv, labels_own,
    tile_send, tile_recv, tile_own, small_sem,
):
    _, bands, _, trip = strength.shape
    pos = position()
    steps = (1, 3, 2)
    slabs = (1, 3, 2, 0)
    fetches = fetch_copies(strength, here, in_sem)
    for fetch in fetches:
        fetch.start()

    barrier = pltpu.get_barrier_semaphore()
    greeted = [(a, r, f) for a in range(3) for r in (1, 2, 3) for f in (False, True)]
    greeted.append((0, 0, True))
    for a, r, f in greeted:
        pl.semaphore_signal(
            barrier, inc=1, device_id=device_at(pos, a, r, f), device_id_type=MESH
        )
    turn_factors(fetches, freqs, here, turned, rows)
    lane = lax.broadcasted_iota(jnp.int32, (1, LANES), 1)

    @pl.loop(0, 2 * SIDE**3, unroll=8)
    def _(o):
        known_here = jnp.where(lane == 0, names[0, o], jnp.where(lane == 1, names[1, o], names[2, 0]))
        labels[lax.div(o, 32), lax.rem(lax.div(o, 8), 4), lax.rem(lax.div(o, 2), 4), lax.rem(o, 2), 0] = (
            known_here
        )

    pl.semaphore_wait(barrier, len(greeted))

    def moved(axis, step):
        return lax.rem(pos[axis] + step, SIDE) if step else pos[axis]

    def compute(x):
        @pl.loop(0, 6)
        def _(i):
            k, half = lax.div(i, 2), lax.rem(i, 2)
            for u in range(8):
                e = k * SIDE**3 + x * SIDE**2 + half * 8 + u
                t = jnp.maximum(cell[e], 0)
                staged[k, x, half * 2 + u // SIDE, u % SIDE] = block_of(
                    turned, rows, trip, bands, t, turn[e]
                )

    def cut(ref, front, p, core, **at):
        index = [core] + [at.get(name, slice(None)) for name in "xyz"]
        return ref.at[(p, *index)] if front else ref.at[(*index, p)]

    def early(stage, p, q):
        axis = (p + stage) % 3
        source, target = ((staged, first), (first, second))[stage]

        def ends(step):
            if axis == 0:
                there, here_at = {"x": moved(0, step)}, {"x": pos[0]}
            else:
                r = slabs[q]
                x = moved(0, (SIDE - r) % SIDE if p == 0 else r)
                there = {"x": x, "xyz"[axis]: moved(axis, step)}
                here_at = {"x": x, "xyz"[axis]: pos[axis]}
            return (
                cut(source, stage > 0, p, slice(None), **there),
                cut(target, True, p, slice(None), **here_at),
            )

        def remote(m, step):
            source_at, target_at = ends(step)
            return pltpu.make_async_remote_copy(
                src_ref=source_at,
                dst_ref=target_at,
                send_sem=send_sem.at[stage, p, q, m],
                recv_sem=recv_sem.at[stage, p, q, m],
                device_id=device_at(pos, axis, step, False),
                device_id_type=MESH,
            )

        def local():
            return pltpu.make_async_copy(*ends(0), own_sem.at[stage, p, q])

        if axis == 0:
            return ([remote(0, slabs[q])], []) if slabs[q] else ([], [local()])
        return [remote(m, step) for m, step in enumerate(steps)], [local()]

    def late(p, f, m):
        axis = (p + 2) % 3
        step = (*steps, 0)[m]
        core = (pos[3], 1 - pos[3], 2)[f]
        there, here_at = {"xyz"[axis]: moved(axis, step)}, {"xyz"[axis]: pos[axis]}
        source = cut(second, True, p, core, **there)
        index = [here_at.get(name, slice(None)) for name in "xyz"]
        if f < 2:
            target = (got_same, got_other)[f].at[(*index, p)]
        else:
            target = got_shared.at[(*index, pos[3], p)]
        if step == 0 and f != 1:
            return pltpu.make_async_copy(source, target, last_own.at[p, f])
        return pltpu.make_async_remote_copy(
            src_ref=source,
            dst_ref=target,
            send_sem=last_send.at[p, f, m],
            recv_sem=last_recv.at[p, f, m],
            device_id=device_at(pos, axis, step, f == 1),
            device_id_type=MESH,
        )

    def is_local(f, m):
        return m == 3 and f != 1

    def pass_on(p):
        mine = got_shared.at[:, :, :, pos[3], p]
        return pltpu.make_async_remote_copy(
            src_ref=mine,
            dst_ref=mine,
            send_sem=last_send.at[p, 3, 0],
            recv_sem=last_recv.at[p, 3, 0],
            device_id=device_at(pos, 0, 0, True),
            device_id_type=MESH,
        )

    def label_messages(stage):
        source, target = (
            (labels, labels_first), (labels_first, labels_second), (labels_second, labels_third)
        )[stage]
        moves = [(r, f) for r in steps for f in (False, True)[: 1 + stage // 2]]
        moves += [(0, True)] if stage == 2 else []

        def ends(step, flip):
            at = [slice(None)] * 4
            to = [slice(None)] * 4
            at[stage], to[stage] = moved(stage, step), pos[stage]
            if stage == 2:
                at[3], to[3] = 1 - pos[3] if flip else pos[3], pos[3]
            return source.at[tuple(at)], target.at[tuple(to)]

        remotes = []
        for m, (step, flip) in enumerate(moves):
            source_at, target_at = ends(step, flip)
            remotes.append(
                pltpu.make_async_remote_copy(
                    src_ref=source_at,
                    dst_ref=target_at,
                    send_sem=labels_send.at[stage, m],
                    recv_sem=labels_recv.at[stage, m],
                    device_id=device_at(pos, stage, step, flip),
                    device_id_type=MESH,
                )
            )
        return remotes, [pltpu.make_async_copy(*ends(0, False), labels_own.at[stage])]

    def start(messages):
        for group in messages:
            for copy in group:
                copy.start()

    def arrive(messages):
        remotes, locals_ = messages
        for copy in remotes:
            copy.wait_recv()
        for copy in locals_:
            copy.wait()

    def order_labels():
        copy = pltpu.make_async_copy(labels_third, known, small_sem)
        copy.start()
        copy.wait()
        sources = 2 * SIDE**3
        n = 2 * sources
        lanes = lax.broadcasted_iota(jnp.int32, (8, n), 1)

        def gather(s, carry):
            keys, bad = carry
            core = lax.rem(s, 2)
            at = (lax.div(s, 32), lax.rem(lax.div(s, 8), 4), lax.rem(lax.div(s, 2), 4), core, 0, 0)
            for r in range(2):
                label = known[(*at, r)]
                label = jnp.where(label < 0, sources, label)
                if r == 0:
                    label = label + jnp.where(core == pos[3], 2, 1) * (sources + 1)
                keys = jnp.where(lanes == s + r * sources, label, keys)
            return keys, jnp.maximum(bad, known[(*at, 2)])

        names_row, bad = lax.fori_loop(
            0, sources, gather, (jnp.zeros((8, n), jnp.int32), jnp.int32(0)), unroll=8
        )
        flag[0] = bad
        row = lax.broadcasted_iota(jnp.int32, (n, n), 0)
        column = lax.broadcasted_iota(jnp.int32, (n, n), 1)
        keys = names_row * n + lanes
        keys_down = keys.T[:, 0:1]
        names_down = names_row.T[:, 0:1]

        def count(mask):
            return jnp.sum(mask.astype(jnp.int32), axis=0, keepdims=True)

        ahead = keys_down < keys[0:1]
        rank = count(ahead)
        earlier = jnp.minimum(count(ahead & (names_down == names_row[0:1])), 1)
        both = jnp.concatenate([rank, earlier] + [rank] * 6, axis=0).T
        found = both[:, 0:1] == column
        index = jnp.where(row < sources, lax.shift_right_logical(row, 1), row - sources)
        table[0:1, :] = jnp.sum(jnp.where(found, index, 0), axis=0, keepdims=True)
        table[1:2, :] = jnp.sum(jnp.where(found, both[:, 1:2], 0), axis=0, keepdims=True)
        for g in range(3):
            name = column + g * (sources + 1)
            end = count(names_down <= name)
            begin = count(names_down < name)
            table[2 + g : 3 + g, :] = jnp.where(end > begin, end - 1, n)
        copy = pltpu.make_async_copy(table, listed, small_sem)
        copy.start()
        copy.wait()

    n_slots = 4 * SIDE**3
    sums = turned.reshape(n_slots + 1, PARTS, bands // PARTS, LANES)

    def sum_group(got, begin, end):
        def add(r, total):
            kept = listed[1, r].astype(jnp.float32)
            at = listed[0, r]
            index = []
            for length in reversed(got.shape[:-3]):
                index.insert(0, jnp.bitwise_and(at, length - 1))
                at = lax.shift_right_logical(at, length.bit_length() - 1)
            total = total * kept + got[tuple(index)].astype(jnp.float32)
            sums[r] = total
            return total

        lax.fori_loop(begin, end, add, jnp.zeros(sums.shape[1:], jnp.float32), unroll=4)

    def sum_part(p):
        @pl.loop(0, n_slots // 2, unroll=8)
        def _(k):
            total = sums[listed[2, k], p] + sums[listed[3, k], p] + sums[listed[4, k], p]
            x, d = lax.rem(k, SIDE), lax.div(k, SIDE)
            staged[lax.rem(d, 2), x, lax.div(d, 8), lax.rem(lax.div(d, 2), SIDE), p] = (
                total.astype(staged.dtype)
            )

    def tile_messages(stage, p, f):
        axis = (p + stage) % 3
        core = 1 - pos[3] if f else pos[3]

        def ends(step):
            there, here_at = {"xyz"[axis]: moved(axis, step)}, {"xyz"[axis]: pos[axis]}
            source = cut((staged, tile_first, tile_second)[stage], stage > 0, p, core, **there)
            if stage < 2:
                return source, cut((tile_first, tile_second)[stage], True, p, core, **here_at)
            index = [here_at.get(name, slice(None)) for name in "xyz"]
            return source, partner_out.at[(*index, pos[3], p)]

        crossing = stage == 2 and f == 1
        remotes = []
        for m, step in enumerate((*steps, 0) if crossing else steps):
            source, target = ends(step)
            remotes.append(
                pltpu.make_async_remote_copy(
                    src_ref=source,
                    dst_ref=target,
                    send_sem=tile_send.at[stage, p, f, m],
                    recv_sem=tile_recv.at[stage, p, f, m],
                    device_id=device_at(pos, axis, step, crossing),
                    device_id_type=MESH,
                )
            )
        if crossing:
            return remotes, []
        return remotes, [pltpu.make_async_copy(*ends(0), tile_own.at[stage, p, f])]

    start(label_messages(0))
    for q in range(SIDE):
        compute(moved(0, slabs[q]))
        for p in range(PARTS):
            start(early(0, p, q))
    arrive(label_messages(0))
    start(label_messages(1))
    for q in range(SIDE):
        for p in range(PARTS):
            arrive(early(0, p, q))
            start(early(1, p, q))
    arrive(label_messages(1))
    start(label_messages(2))
    for q in range(SIDE):
        arrive(early(1, 1, q))
        m = (*steps, 0).index(slabs[q])
        for f in (2, 1, 0):
            late(1, f, m).start()
    for p in (0, 2):
        for q in range(SIDE):
            arrive(early(1, p, q))
        for f in (2, 1, 0):
            for m in range(4):
                late(p, f, m).start()
    arrive(label_messages(2))
    order_labels()
    sums[n_slots] = jnp.zeros(sums.shape[1:], jnp.float32)

    def arrive_late(p, f):
        for m in range(4):
            if is_local(f, m):
                late(p, f, m).wait()
            else:
                late(p, f, m).wait_recv()

    for p in (1, 0, 2):
        arrive_late(p, 2)
        pass_on(p).start()
    for p in (1, 0, 2):
        arrive_late(p, 1)
    sum_group(got_other, n_slots // 2, n_slots * 3 // 4)
    for p in (1, 0, 2):
        pass_on(p).wait_recv()
    sum_group(got_shared, 0, n_slots // 2)
    for stage in range(2):
        for p in range(PARTS):
            for q in range(SIDE):
                for copy in early(stage, p, q)[0]:
                    copy.wait_send()
    for p in (1, 0, 2):
        arrive_late(p, 0)
    sum_group(got_same, n_slots * 3 // 4, n_slots)
    tile_jobs = [(p, f) for p in (1, 0, 2) for f in (1, 0)]
    for p in (1, 0, 2):
        sum_part(p)
        for f in (1, 0):
            start(tile_messages(0, p, f))
    keep = pltpu.make_async_copy(staged.at[0:2], omega_out, small_sem)
    keep.start()
    for stage in (1, 2):
        for job in tile_jobs:
            arrive(tile_messages(stage - 1, *job))
            start(tile_messages(stage, *job))
    for p in range(PARTS):
        pass_on(p).wait_send()
        for f in range(3):
            for m in range(4):
                if not is_local(f, m):
                    late(p, f, m).wait_send()
    for stage in range(3):
        for copy in label_messages(stage)[0]:
            copy.wait_send()
    for job in tile_jobs:
        arrive(tile_messages(2, *job))
    keep.wait()
    for stage in range(3):
        for job in tile_jobs:
            for copy in tile_messages(stage, *job)[0]:
                copy.wait_send()


def sums_and_partners(cell, turn, labels, strength, freqs, collective_id):
    _, bands, _, trip = strength.shape
    part = (bands // PARTS, LANES)
    torus = (SIDE, SIDE, SIDE)
    moving = pltpu.VMEM((PARTS, 3, *torus, *part), jnp.bfloat16)
    moving_tiles = pltpu.VMEM((PARTS, 2, *torus, *part), jnp.bfloat16)
    smem = pl.BlockSpec(memory_space=pltpu.SMEM)
    anywhere = pl.BlockSpec(memory_space=pl.ANY)
    label_rows = (*torus, 2, 1, 1, LANES)
    moving_labels = pltpu.VMEM(label_rows, jnp.int32)
    dma = pltpu.SemaphoreType.DMA
    slots = 4 * SIDE**3
    return pl.pallas_call(
        main_kernel,
        name="sums_and_partners",
        out_shape=[
            jax.ShapeDtypeStruct((2, *torus, PARTS, *part), jnp.bfloat16),
            jax.ShapeDtypeStruct((*torus, 2, PARTS, *part), jnp.bfloat16),
            jax.ShapeDtypeStruct((1,), jnp.int32),
        ],
        in_specs=[smem, smem, smem, anywhere, pl.BlockSpec(memory_space=pltpu.VMEM)],
        out_specs=[anywhere, anywhere, smem],
        scratch_shapes=[
            pltpu.VMEM(strength.shape, strength.dtype),
            pltpu.VMEM((2 * trip + 1, bands, LANES), jnp.float32),
            pltpu.VMEM((2 * trip, 8, LANES), jnp.float32),
            pltpu.VMEM((3, *torus, PARTS, *part), jnp.bfloat16),
            moving,
            moving,
            pltpu.VMEM((*torus, PARTS, *part), jnp.bfloat16),
            pltpu.VMEM((*torus, PARTS, *part), jnp.bfloat16),
            pltpu.VMEM((*torus, 2, PARTS, *part), jnp.bfloat16),
            moving_tiles,
            moving_tiles,
            moving_labels,
            moving_labels,
            moving_labels,
            moving_labels,
            pltpu.SMEM(label_rows, jnp.int32),
            pltpu.VMEM((8, slots), jnp.int32),
            pltpu.SMEM((8, slots), jnp.int32),
            dma((PIECES,)),
            dma((2, PARTS, SIDE, 3)),
            dma((2, PARTS, SIDE, 3)),
            dma((2, PARTS, SIDE)),
            dma((PARTS, 4, 4)),
            dma((PARTS, 4, 4)),
            dma((PARTS, 3)),
            dma((3, 7)),
            dma((3, 7)),
            dma((3,)),
            dma((3, PARTS, 2, 4)),
            dma((3, PARTS, 2, 4)),
            dma((3, PARTS, 2)),
            dma,
        ],
        compiler_params=pltpu.CompilerParams(
            collective_id=collective_id, has_side_effects=True, vmem_limit_bytes=60 * 2**20
        ),
    )(cell, turn, labels, strength, freqs)


def sum_kernel(labels, one, two, out, total):
    step = pl.program_id(0)
    here = one.shape[0]
    tiles = out.shape[0]

    @pl.when(step == 0)
    def _():
        @pl.loop(0, tiles, unroll=4)
        def _(k):
            total[k] = jnp.zeros(total.shape[1:], jnp.float32)

    @pl.loop(0, here, unroll=4)
    def _(s):
        for r, got in enumerate((one, two)):
            label = labels[step * here + s, r]
            total[jnp.where(label < 0, tiles, label)] += got[s].astype(jnp.float32)

    @pl.when(step == pl.num_programs(0) - 1)
    def _():
        @pl.loop(0, tiles, unroll=4)
        def _(k):
            out[k] = total[k].astype(out.dtype)


def sum_tiles(labels, one, two, tiles):
    devices, *part = one.shape
    here = 32
    spec = pl.BlockSpec((here, *part), lambda i: (i, 0, 0, 0))
    return pl.pallas_call(
        sum_kernel,
        name="sum_tiles",
        grid=(devices // here,),
        out_shape=jax.ShapeDtypeStruct((tiles, *part), jnp.bfloat16),
        in_specs=[pl.BlockSpec(memory_space=pltpu.SMEM), spec, spec],
        out_specs=pl.BlockSpec(memory_space=pltpu.VMEM),
        scratch_shapes=[pltpu.VMEM((tiles + 1, *part), jnp.float32)],
        compiler_params=pltpu.CompilerParams(vmem_limit_bytes=VMEM_BYTES),
    )(labels, one, two)


def symmetrize_kernel(omega, partner, out):
    *_, thirds, part, lanes = omega.shape
    bands = thirds * part
    for z in range(SIDE):
        for core in range(2):
            for x in range(SIDE):
                mine = omega[core, x, 0, z].astype(jnp.float32).reshape(bands, lanes)
                other = partner[x, 0, z, core].astype(jnp.float32).reshape(bands, lanes).T
                out[z * 2 + core, pl.ds(x, bands, stride=SIDE), :] = 0.5 * (
                    mine[:, 0:bands] + other[0:bands]
                )


def symmetrize(omega, partner):
    *_, thirds, part, lanes = omega.shape
    bands = thirds * part
    rest = (thirds, part, lanes)
    rows = 2 * SIDE
    return pl.pallas_call(
        symmetrize_kernel,
        name="symmetrize",
        grid=(SIDE,),
        out_shape=jax.ShapeDtypeStruct((rows * SIDE, bands * SIDE, bands), jnp.float32),
        in_specs=[
            pl.BlockSpec((2, SIDE, 1, SIDE, *rest), lambda y: (0, 0, y, 0, 0, 0, 0)),
            pl.BlockSpec((SIDE, 1, SIDE, 2, *rest), lambda y: (0, y, 0, 0, 0, 0, 0)),
        ],
        out_specs=pl.BlockSpec((rows, bands * SIDE, bands), lambda y: (y, 0, 0)),
        compiler_params=pltpu.CompilerParams(vmem_limit_bytes=60 * 2**20),
    )(omega, partner)


def per_device(strength, freqs, owner, tile_slot, live_count):
    bands = strength.shape[2]
    n_grp = lax.axis_size("grp")
    n_dev = lax.axis_size("dev")
    grid = (n_grp, n_dev)
    devices = n_grp * n_dev
    part = (PARTS, bands // PARTS, LANES)
    torus = (SIDE, SIDE, SIDE)
    plain = ((0, 1, 2, 3), (0, 1, 2, 3))
    by_lane, freqs = strength.transpose(1, 2, 3, 0), freqs.transpose(1, 2, 0)
    names = (owner[:, 0], tile_slot, live_count)

    def with_labels(labels):
        return labels.reshape(*torus, 2, 1, 1, LANES)

    cell, turn, labels = make_plan(*names, grid)
    omega, partner, flag = sums_and_partners(
        cell, turn, labels, by_lane, freqs, 1
    )

    def main():
        return symmetrize(omega, partner)

    def dense():
        cells, labels = dense_blocks(by_lane, freqs, *names, grid)
        cells = cells.reshape(2, 2, *torus, *part)
        moved = ((1, 2, 3, 0), (0, 1, 2, 3))
        one, two, labels = exchange(
            [cells[0], cells[1], with_labels(labels)], [moved, moved, plain], 3, "send_dense"
        )
        omega = sum_tiles(
            labels.reshape(devices, LANES),
            one.reshape(devices, *part),
            two.reshape(devices, *part),
            devices,
        )
        omega = omega.reshape(SIDE, SIDE, 2, n_grp, *part).transpose(2, 3, 0, 1, 4, 5, 6)
        (partner,) = exchange([omega], [moved], 2, "send_tiles")
        return symmetrize(omega, partner)

    sym = lax.cond(flag[0] > 0, dense, main)
    return sym.reshape(devices // n_grp, bands, n_grp, 1, bands)


def solution(mesh):
    return jax.shard_map(
        per_device,
        mesh=mesh,
        in_specs=(
            P(("grp", "dev"), None, None, None),
            P(("grp", "dev"), None, None),
            P(("grp", "dev"), None),
            P(("grp", "dev")),
            P(("grp", "dev")),
        ),
        out_specs=P("grp", None, None, "dev", None),
        check_vma=False,
    )
```

```python
import functools

import jax
import jax.numpy as jnp
from jax import lax
from jax.experimental import pallas as pl
from jax.experimental.pallas import tpu as pltpu
from jax.sharding import PartitionSpec as P

MESH = pl.DeviceIdType.MESH
LANES = 128
SIDE = 4
VMEM_BYTES = 56 * 2**20


PARTS = 3
WALK = 400
PIECES = 12
HEIGHTS = (24, 16)


def position():
    g, d = lax.axis_index("grp"), lax.axis_index("dev")
    return g, d // 8, lax.rem(d // 2, 4), lax.rem(d, 2)


def device_at(pos, axis, step, flip):
    at = list(pos)
    if step:
        at[axis] = lax.rem(pos[axis] + step, SIDE)
    if flip:
        at[3] = 1 - pos[3]
    return at[0], (at[1] * SIDE + at[2]) * 2 + at[3]


def exchange_kernel(plans, *refs):
    n = len(plans)
    srcs, dsts, firsts, seconds = (refs[k * n : (k + 1) * n] for k in range(4))
    send_sem, recv_sem, own_sem = refs[4 * n :]
    pos = position()
    steps = (1, 3, 2)

    barrier = pltpu.get_barrier_semaphore()
    greeted = [(a, r, f) for a in range(3) for r in (1, 2, 3) for f in (False, True)]
    greeted.append((0, 0, True))
    for a, r, f in greeted:
        pl.semaphore_signal(
            barrier, inc=1, device_id=device_at(pos, a, r, f), device_id_type=MESH
        )
    pl.semaphore_wait(barrier, len(greeted))

    def view(ref, places, front, p, axis, at, core):
        index = [slice(None)] * 4
        index[places[axis]] = at
        index[places[3]] = core
        return ref.at[(p,) + tuple(index)] if front else ref.at[tuple(index) + (p,)]

    def ends(stage, k, f, p, step):
        src_places, dst_places = plans[k]
        axis = (p + stage) % 3
        there = lax.rem(pos[axis] + step, SIDE) if step else pos[axis]
        core = (pos[3], 1 - pos[3])[f]
        source = view((srcs, firsts, seconds)[stage][k], src_places, stage > 0, p, axis, there, core)
        if stage < 2:
            target = view((firsts, seconds)[stage][k], src_places, True, p, axis, pos[axis], core)
        else:
            target = view(dsts[k], dst_places, False, p, axis, pos[axis], pos[3])
        return source, target

    def remote(stage, k, f, p, m):
        step = (*steps, 0)[m]
        source, target = ends(stage, k, f, p, step)
        return pltpu.make_async_remote_copy(
            src_ref=source,
            dst_ref=target,
            send_sem=send_sem.at[stage, k, f, p, m],
            recv_sem=recv_sem.at[stage, k, f, p, m],
            device_id=device_at(pos, (p + stage) % 3, step, stage == 2 and f == 1),
            device_id_type=MESH,
        )

    def copies(stage, k, f, p):
        if stage == 2 and f == 1:
            return [remote(stage, k, f, p, m) for m in range(4)], []
        source, target = ends(stage, k, f, p, 0)
        return (
            [remote(stage, k, f, p, m) for m in range(3)],
            [pltpu.make_async_copy(source, target, own_sem.at[stage, k, f, p])],
        )

    def start(*job):
        for group in copies(*job):
            for copy in group:
                copy.start()

    def arrive(*job):
        remotes, locals_ = copies(*job)
        for copy in remotes:
            copy.wait_recv()
        for copy in locals_:
            copy.wait()

    jobs = [
        (k, f, p)
        for f in (1, 0)
        for p in range(PARTS)
        for k in range(n)
        if p < firsts[k].shape[0]
    ]
    for job in jobs:
        start(0, *job)
    for stage in (1, 2):
        for job in jobs:
            arrive(stage - 1, *job)
            start(stage, *job)
    for job in jobs:
        arrive(2, *job)
    for stage in range(3):
        for job in jobs:
            for copy in copies(stage, *job)[0]:
                copy.wait_send()


def exchange(arrays, plans, collective_id, name):
    n = len(arrays)
    outs, temps = [], []
    for a, (src_places, dst_places) in zip(arrays, plans):
        front = [0] * 4
        for axis in range(4):
            front[dst_places[axis]] = a.shape[src_places[axis]]
        rest = a.shape[4:]
        outs.append(jax.ShapeDtypeStruct((*front, *rest), a.dtype))
        temps.append(pltpu.VMEM((rest[0],) + a.shape[:4] + rest[1:], a.dtype))
    anywhere = pl.BlockSpec(memory_space=pl.ANY)
    return pl.pallas_call(
        functools.partial(exchange_kernel, plans),
        name=name,
        out_shape=outs,
        in_specs=[anywhere] * n,
        out_specs=[anywhere] * n,
        scratch_shapes=temps
        + temps
        + [pltpu.SemaphoreType.DMA((3, n, 2, PARTS, 4))] * 2
        + [pltpu.SemaphoreType.DMA((3, n, 2, PARTS))],
        compiler_params=pltpu.CompilerParams(
            collective_id=collective_id, has_side_effects=True, vmem_limit_bytes=VMEM_BYTES
        ),
    )(*arrays)


def plan_kernel(grid, owner, tile, live, cell, turn, labels, left):
    n_grp, n_dev = grid
    devices = n_grp * n_dev
    chips = devices // 2

    @pl.loop(0, devices, unroll=8)
    def _(o):
        labels[0, o] = -1
        labels[1, o] = -1

    @pl.loop(0, cell.shape[0], unroll=8)
    def _(e):
        cell[e] = -1
        turn[e] = 0

    def first(t, n):
        o = owner[t]
        e = lax.rem(o, 2) * chips + lax.div(o, 2)
        held = cell[e]
        taken = held >= 0
        cell[e] = jnp.where(taken, held, t)
        labels[0, o] = jnp.where(taken, labels[0, o], tile[t])
        left[n] = t
        return n + taken.astype(jnp.int32)

    n_left = lax.fori_loop(0, live[0], first, jnp.int32(0))

    def insert(q, carry):
        lost, noise = carry

        def body(state):
            t, steps, noise = state
            o, k = owner[t], tile[t]
            x = lax.rem(k, n_grp) * n_dev + lax.div(k, n_grp)
            e0 = lax.rem(o, 2) * chips + lax.div(o, 2)
            e1 = devices + lax.div(o, 2)
            e2 = lax.rem(x, 2) * chips + lax.div(x, 2)
            e3 = devices + lax.div(x, 2)
            noise = lax.rem(noise * 1103 + 12345, 65521)
            pick = lax.rem(lax.div(noise, 8), 4)
            for r, e in ((3, e3), (2, e2), (0, e0), (1, e1)):
                pick = jnp.where(cell[e] < 0, r, pick)
            e = jnp.where(pick == 0, e0, jnp.where(pick == 1, e1, jnp.where(pick == 2, e2, e3)))
            turned = pick >= 2
            to = jnp.where(turned, x, o)
            label = jnp.where(turned, lax.rem(o, n_dev) * n_grp + lax.div(o, n_dev), k)
            victim = cell[e]
            cell[e] = t
            turn[e] = turned.astype(jnp.int32)
            both = (e >= devices).astype(jnp.int32)
            labels[both, to] = label

            @pl.when(e >= devices)
            def _():
                labels[1, to + 1 - 2 * lax.rem(to, 2)] = -1

            return victim, steps + 1, noise

        t, _, noise = lax.while_loop(
            lambda state: (state[0] >= 0) & (state[1] < WALK), body, (left[q], 0, noise)
        )
        return lost | (t >= 0).astype(jnp.int32), noise

    lost, _ = lax.fori_loop(0, n_left, insert, (jnp.int32(0), jnp.int32(1)))

    labels[2, 0] = lost


def make_plan(owner, tile, live, grid):
    devices = grid[0] * grid[1]
    smem = pl.BlockSpec(memory_space=pltpu.SMEM)
    cells = jax.ShapeDtypeStruct((devices * 3 // 2,), jnp.int32)
    return pl.pallas_call(
        functools.partial(plan_kernel, grid),
        name="plan",
        out_shape=[cells, cells, jax.ShapeDtypeStruct((3, devices), jnp.int32)],
        in_specs=[smem] * 3,
        out_specs=[smem] * 3,
        scratch_shapes=[pltpu.SMEM((tile.shape[0] + 1,), jnp.int32)],
    )(owner, tile, live)


def fetch_copies(strength, here, in_sem):
    pieces = in_sem.shape[0]
    piece = strength.shape[1] // pieces
    return [
        pltpu.make_async_copy(
            strength.at[:, pl.ds(i * piece, piece)],
            here.at[:, pl.ds(i * piece, piece)],
            in_sem.at[i],
        )
        for i in range(pieces)
    ]


def turn_factors(fetches, freqs, here, turned, rows):
    _, bands, _, trip = here.shape
    flat = turned.reshape(turned.shape[0] * bands, LANES)
    flat_rows = rows.reshape(2 * trip * 8, LANES)
    lines = []
    for mode in (0, 1):
        occ = 1.0 / (jnp.exp(freqs[mode]) - 1.0)
        lines.append((freqs[mode].T, jnp.sqrt(occ * (occ + 1.0)).T))
    for f in (0, 1):
        for q, value in enumerate(lines[f] + lines[1 - f]):
            flat_rows[pl.ds(f * trip * 8 + q, trip, stride=8), 0:bands] = value
    third = 1.0 / (jnp.exp(freqs[2]) - 1.0) + 1.0
    eye = (
        lax.broadcasted_iota(jnp.int32, (trip, trip), 0)
        == lax.broadcasted_iota(jnp.int32, (trip, trip), 1)
    ).astype(jnp.bfloat16)
    piece = bands // len(fetches)
    for i, fetch in enumerate(fetches):
        fetch.wait()

        @pl.loop(i * piece, (i + 1) * piece, unroll=10)
        def _(j):
            scaled = (here[0, j].astype(jnp.float32) * third).astype(jnp.bfloat16)
            flat[pl.ds(j, trip, stride=bands), 0:bands] = scaled.T.astype(jnp.float32)
            other = lax.dot_general(
                eye, here[1, j], (((1,), (1,)), ((), ())), preferred_element_type=jnp.float32
            )
            flat[pl.ds(trip * bands + j, trip, stride=bands), 0:bands] = other


def block_of(turned, rows, trip, bands, t, f):
    factors = [
        turned[h * trip + t][:, 0:bands].astype(jnp.bfloat16) for h in (f, 1 - f)
    ]
    core = lax.dot_general(
        *factors, (((1,), (1,)), ((), ())), preferred_element_type=jnp.float32
    )
    line = rows[f * trip + t]
    column = line.T[0:bands]
    diff = column[:, 0:1] - line[2:3, 0:bands]
    scale = column[:, 1:2] * line[3:4, 0:bands] * jnp.exp(-diff * diff / 0.5)
    return jnp.pad(scale * core, ((0, 0), (0, LANES - bands)))


def dense_kernel(
    grid, owner, tile, live, strength, freqs, out, labels,
    here, turned, rows, block, cell, place, in_sem, out_sem,
):
    _, bands, _, trip = strength.shape
    devices = grid[0] * grid[1]
    chips = devices // 2
    fetches = fetch_copies(strength, here, in_sem)
    for fetch in fetches:
        fetch.start()

    @pl.loop(0, devices)
    def _(o):
        labels[o, 0] = -1
        labels[o, 1] = -1
        cell[o] = 0

    @pl.loop(0, trip)
    def _(t):
        place[t] = -1

    @pl.loop(0, live[0])
    def _(t):
        o = owner[t]
        r = cell[o]
        cell[o] = r + 1
        place[t] = (r * 2 + lax.rem(o, 2)) * chips + lax.div(o, 2)
        labels[o, r] = tile[t]

    turn_factors(fetches, freqs, here, turned, rows)

    def send(t):
        return pltpu.make_async_copy(block.at[t], out.at[place[t]], out_sem)

    @pl.loop(0, trip)
    def _(t):
        value = block_of(turned, rows, trip, bands, t, 0)
        block[t] = value.reshape(block.shape[1:]).astype(block.dtype)

        @pl.when(place[t] >= 0)
        def _():
            send(t).start()

    @pl.loop(0, trip)
    def _(t):
        @pl.when(place[t] >= 0)
        def _():
            send(t).wait()


def dense_blocks(strength, freqs, owner, tile, live, grid):
    _, bands, _, trip = strength.shape
    devices = grid[0] * grid[1]
    smem = pl.BlockSpec(memory_space=pltpu.SMEM)
    anywhere = pl.BlockSpec(memory_space=pl.ANY)
    part = (PARTS, bands // PARTS, LANES)
    return pl.pallas_call(
        functools.partial(dense_kernel, grid),
        name="dense_blocks",
        out_shape=[
            jax.ShapeDtypeStruct((devices * 2, *part), jnp.bfloat16),
            jax.ShapeDtypeStruct((devices, LANES), jnp.int32),
        ],
        in_specs=[smem, smem, smem, anywhere, pl.BlockSpec(memory_space=pltpu.VMEM)],
        out_specs=[anywhere, smem],
        scratch_shapes=[
            pltpu.VMEM(strength.shape, strength.dtype),
            pltpu.VMEM((2 * trip, bands, LANES), jnp.float32),
            pltpu.VMEM((2 * trip, 8, LANES), jnp.float32),
            pltpu.VMEM((trip, *part), jnp.bfloat16),
            pltpu.SMEM((devices,), jnp.int32),
            pltpu.SMEM((trip,), jnp.int32),
            pltpu.SemaphoreType.DMA((PIECES,)),
            pltpu.SemaphoreType.DMA,
        ],
        compiler_params=pltpu.CompilerParams(vmem_limit_bytes=VMEM_BYTES),
    )(owner, tile, live, strength, freqs)


def main_kernel(cell, turn, names, strength, freqs, *refs):
    omega_out, partner_out, refs = refs[:2], refs[2:4], refs[4:]
    flag, here, turned, rows, refs = *refs[:4], refs[4:]
    staged, first, second, got_same, got_other, got_shared, tile_first, tile_second = (
        refs[2 * r : 2 * r + 2] for r in range(8)
    )
    labels, labels_first, labels_second, labels_third, known, table, listed, *refs = refs[16:]
    in_sem, send_sem, recv_sem, own_sem, last_send, last_recv, last_own, *refs = refs
    labels_send, labels_recv, labels_own, tile_send, tile_recv, tile_own, small_sem, keep_sem = refs
    _, bands, _, trip = strength.shape
    pos = position()
    steps = (1, 3, 2)
    slabs = (1, 3, 2, 0)
    sets = (0, 1)
    fetches = fetch_copies(strength, here, in_sem)
    for fetch in fetches:
        fetch.start()

    barrier = pltpu.get_barrier_semaphore()
    greeted = [(a, r, f) for a in range(3) for r in (1, 2, 3) for f in (False, True)]
    greeted.append((0, 0, True))
    for a, r, f in greeted:
        pl.semaphore_signal(
            barrier, inc=1, device_id=device_at(pos, a, r, f), device_id_type=MESH
        )
    turn_factors(fetches, freqs, here, turned, rows)
    lane = lax.broadcasted_iota(jnp.int32, (1, LANES), 1)

    @pl.loop(0, 2 * SIDE**3, unroll=8)
    def _(o):
        known_here = jnp.where(lane == 0, names[0, o], jnp.where(lane == 1, names[1, o], names[2, 0]))
        labels[lax.div(o, 32), lax.rem(lax.div(o, 8), 4), lax.rem(lax.div(o, 2), 4), lax.rem(o, 2), 0] = (
            known_here
        )

    pl.semaphore_wait(barrier, len(greeted))

    def moved(axis, step):
        return lax.rem(pos[axis] + step, SIDE) if step else pos[axis]

    def compute(x):
        @pl.loop(0, 6)
        def _(i):
            k, half = lax.div(i, 2), lax.rem(i, 2)
            for u in range(8):
                e = k * SIDE**3 + x * SIDE**2 + half * 8 + u
                t = jnp.maximum(cell[e], 0)
                value = block_of(turned, rows, trip, bands, t, turn[e])
                begin = 0
                for h in sets:
                    shape = staged[h].shape[4:]
                    end = begin + shape[0] * shape[1]
                    staged[h][k, x, half * 2 + u // SIDE, u % SIDE] = (
                        value[begin:end].reshape(shape).astype(staged[h].dtype)
                    )
                    begin = end

    def cut(ref, front, p, core, **at):
        index = [core] + [at.get(name, slice(None)) for name in "xyz"]
        return ref.at[(p, *index)] if front else ref.at[(*index, p)]

    def early(stage, h, p, q=None):
        axis = (p + stage) % 3
        source, target = ((staged, first), (first, second))[stage]

        def ends(step):
            there, here_at = {"xyz"[axis]: moved(axis, step)}, {"xyz"[axis]: pos[axis]}
            if axis and q is not None:
                there["x"] = here_at["x"] = moved(0, slabs[q])
            return (
                cut(source[h], stage > 0, p, slice(None), **there),
                cut(target[h], True, p, slice(None), **here_at),
            )

        def remote(m, step):
            source_at, target_at = ends(step)
            at = (stage, h, p, q or 0, m)
            return pltpu.make_async_remote_copy(
                src_ref=source_at,
                dst_ref=target_at,
                send_sem=send_sem.at[at],
                recv_sem=recv_sem.at[at],
                device_id=device_at(pos, axis, step, False),
                device_id_type=MESH,
            )

        local = [pltpu.make_async_copy(*ends(0), own_sem.at[stage, h, p, q or 0])]
        if axis == 0 and q is not None:
            return ([remote(0, slabs[q])], []) if slabs[q] else ([], local)
        return [remote(m, step) for m, step in enumerate(steps)], local

    def late(h, p, f):
        axis = (p + 2) % 3
        core = (pos[3], 1 - pos[3], 2)[f]

        def ends(step):
            source = cut(second[h], True, p, core, **{"xyz"[axis]: moved(axis, step)})
            index = [slice(None)] * 3
            index[axis] = pos[axis]
            if f == 2:
                return source, got_shared[h].at[(*index, pos[3], p)]
            return source, (got_same, got_other)[f][h].at[(*index, p)]

        remotes = []
        for m, step in enumerate((*steps, 0) if f == 1 else steps):
            source, target = ends(step)
            remotes.append(
                pltpu.make_async_remote_copy(
                    src_ref=source,
                    dst_ref=target,
                    send_sem=last_send.at[h, p, f, m],
                    recv_sem=last_recv.at[h, p, f, m],
                    device_id=device_at(pos, axis, step, f == 1),
                    device_id_type=MESH,
                )
            )
        if f == 1:
            return remotes, []
        return remotes, [pltpu.make_async_copy(*ends(0), last_own.at[h, p, f])]

    def pass_on(h, p):
        mine = got_shared[h].at[:, :, :, pos[3], p]
        return pltpu.make_async_remote_copy(
            src_ref=mine,
            dst_ref=mine,
            send_sem=last_send.at[h, p, 3, 0],
            recv_sem=last_recv.at[h, p, 3, 0],
            device_id=device_at(pos, 0, 0, True),
            device_id_type=MESH,
        )

    def label_messages(stage):
        source, target = (
            (labels, labels_first), (labels_first, labels_second), (labels_second, labels_third)
        )[stage]
        moves = [(r, f) for r in steps for f in (False, True)[: 1 + stage // 2]]
        moves += [(0, True)] if stage == 2 else []

        def ends(step, flip):
            at = [slice(None)] * 4
            to = [slice(None)] * 4
            at[stage], to[stage] = moved(stage, step), pos[stage]
            if stage == 2:
                at[3], to[3] = 1 - pos[3] if flip else pos[3], pos[3]
            return source.at[tuple(at)], target.at[tuple(to)]

        remotes = []
        for m, (step, flip) in enumerate(moves):
            source_at, target_at = ends(step, flip)
            remotes.append(
                pltpu.make_async_remote_copy(
                    src_ref=source_at,
                    dst_ref=target_at,
                    send_sem=labels_send.at[stage, m],
                    recv_sem=labels_recv.at[stage, m],
                    device_id=device_at(pos, stage, step, flip),
                    device_id_type=MESH,
                )
            )
        return remotes, [pltpu.make_async_copy(*ends(0, False), labels_own.at[stage])]

    def start(messages):
        for group in messages:
            for copy in group:
                copy.start()

    def arrive(messages):
        remotes, locals_ = messages
        for copy in remotes:
            copy.wait_recv()
        for copy in locals_:
            copy.wait()

    def order_labels():
        copy = pltpu.make_async_copy(labels_third, known, small_sem)
        copy.start()
        copy.wait()
        sources = 2 * SIDE**3
        n = 2 * sources
        lanes = lax.broadcasted_iota(jnp.int32, (8, n), 1)

        def gather(s, carry):
            keys, bad = carry
            core = lax.rem(s, 2)
            at = (lax.div(s, 32), lax.rem(lax.div(s, 8), 4), lax.rem(lax.div(s, 2), 4), core, 0, 0)
            for r in range(2):
                label = known[(*at, r)]
                label = jnp.where(label < 0, sources, label)
                if r == 0:
                    label = label + jnp.where(core == pos[3], 2, 1) * (sources + 1)
                keys = jnp.where(lanes == s + r * sources, label, keys)
            return keys, jnp.maximum(bad, known[(*at, 2)])

        names_row, bad = lax.fori_loop(
            0, sources, gather, (jnp.zeros((8, n), jnp.int32), jnp.int32(0)), unroll=8
        )
        flag[0] = bad
        row = lax.broadcasted_iota(jnp.int32, (n, n), 0)
        column = lax.broadcasted_iota(jnp.int32, (n, n), 1)
        keys = names_row * n + lanes
        keys_down = keys.T[:, 0:1]
        names_down = names_row.T[:, 0:1]

        def count(mask):
            return jnp.sum(mask.astype(jnp.int32), axis=0, keepdims=True)

        ahead = keys_down < keys[0:1]
        rank = count(ahead)
        earlier = jnp.minimum(count(ahead & (names_down == names_row[0:1])), 1)
        both = jnp.concatenate([rank, earlier] + [rank] * 6, axis=0).T
        found = both[:, 0:1] == column
        index = jnp.where(row < sources, lax.shift_right_logical(row, 1), row - sources)
        table[0:1, :] = jnp.sum(jnp.where(found, index, 0), axis=0, keepdims=True)
        table[1:2, :] = jnp.sum(jnp.where(found, both[:, 1:2], 0), axis=0, keepdims=True)
        for g in range(3):
            name = column + g * (sources + 1)
            end = count(names_down <= name)
            begin = count(names_down < name)
            table[2 + g : 3 + g, :] = jnp.where(end > begin, end - 1, n)
        copy = pltpu.make_async_copy(table, listed, small_sem)
        copy.start()
        copy.wait()

    n_slots = 4 * SIDE**3
    sums = turned.reshape(n_slots + 1, bands // 8, 8, LANES)
    tile_rows = [staged[h].shape[4] * staged[h].shape[5] // 8 for h in sets]
    spans = [slice(0, tile_rows[0]), slice(tile_rows[0], sum(tile_rows))]

    def sum_group(h, got, begin, end):
        def add(r, total):
            kept = listed[1, r].astype(jnp.float32)
            at = listed[0, r]
            index = []
            for length in reversed(got.shape[:-3]):
                index.insert(0, jnp.bitwise_and(at, length - 1))
                at = lax.shift_right_logical(at, length.bit_length() - 1)
            block = got[tuple(index)].astype(jnp.float32).reshape(total.shape)
            total = total * kept + block
            sums[r, spans[h]] = total
            return total

        lax.fori_loop(
            begin, end, add, jnp.zeros((tile_rows[h], 8, LANES), jnp.float32), unroll=4
        )

    def sum_part(h, p):
        _, height, _ = staged[h].shape[4:]
        begin = spans[h].start + p * height // 8
        span = slice(begin, begin + height // 8)

        @pl.loop(0, n_slots // 2, unroll=8)
        def _(k):
            total = sums[listed[2, k]][span] + sums[listed[3, k]][span] + sums[listed[4, k]][span]
            x, d = lax.rem(k, SIDE), lax.div(k, SIDE)
            staged[h][lax.rem(d, 2), x, lax.div(d, 8), lax.rem(lax.div(d, 2), SIDE), p] = (
                total.reshape(height, LANES).astype(staged[h].dtype)
            )

    def tile_messages(stage, h, p, f=None):
        axis = (p + stage) % 3
        core = slice(0, 2) if f is None else (1 - pos[3] if f else pos[3])

        def ends(step):
            there, here_at = {"xyz"[axis]: moved(axis, step)}, {"xyz"[axis]: pos[axis]}
            source = cut((staged, tile_first, tile_second)[stage][h], stage > 0, p, core, **there)
            if stage < 2:
                return source, cut((tile_first, tile_second)[stage][h], True, p, core, **here_at)
            index = [here_at.get(name, slice(None)) for name in "xyz"]
            return source, partner_out[h].at[(*index, pos[3], p)]

        remotes = []
        for m, step in enumerate((*steps, 0) if f else steps):
            source, target = ends(step)
            at = (stage, h, p, f or 0, m)
            remotes.append(
                pltpu.make_async_remote_copy(
                    src_ref=source,
                    dst_ref=target,
                    send_sem=tile_send.at[at],
                    recv_sem=tile_recv.at[at],
                    device_id=device_at(pos, axis, step, bool(f)),
                    device_id_type=MESH,
                )
            )
        if f:
            return remotes, []
        return remotes, [pltpu.make_async_copy(*ends(0), tile_own.at[stage, h, p])]

    start(label_messages(0))
    for q in range(SIDE):
        compute(moved(0, slabs[q]))
        for p in range(PARTS):
            start(early(0, 0, p, q))
    for p in range(PARTS):
        start(early(0, 1, p))
    arrive(label_messages(0))
    start(label_messages(1))
    for p in range(PARTS):
        for q in range(SIDE):
            remotes, local = early(0, 0, p, q)
            arrive((remotes, local))
        start(early(1, 0, p))
    for p in range(PARTS):
        arrive(early(0, 1, p))
        start(early(1, 1, p))
    arrive(label_messages(1))
    start(label_messages(2))
    for h in sets:
        for p in range(PARTS):
            arrive(early(1, h, p))
            for f in (2, 1, 0):
                start(late(h, p, f))
    arrive(label_messages(2))
    order_labels()
    sums[n_slots] = jnp.zeros(sums.shape[1:], jnp.float32)
    keeps = [
        pltpu.make_async_copy(staged[h].at[0:2], omega_out[h], keep_sem.at[h]) for h in sets
    ]
    for h in sets:
        for p in range(PARTS):
            arrive(late(h, p, 2))
            pass_on(h, p).start()
        for p in range(PARTS):
            arrive(late(h, p, 1))
        sum_group(h, got_other[h], n_slots // 2, n_slots * 3 // 4)
        for p in range(PARTS):
            pass_on(h, p).wait_recv()
        sum_group(h, got_shared[h], 0, n_slots // 2)
        for p in range(PARTS):
            for q in [None] if h else range(SIDE):
                for copy in early(0, h, p, q)[0]:
                    copy.wait_send()
        for p in range(PARTS):
            arrive(late(h, p, 0))
        sum_group(h, got_same[h], n_slots * 3 // 4, n_slots)
        for p in range(PARTS):
            sum_part(h, p)
            start(tile_messages(0, h, p))
        keeps[h].start()
    for h in sets:
        for p in range(PARTS):
            arrive(tile_messages(0, h, p))
            start(tile_messages(1, h, p))
    for h in sets:
        for p in range(PARTS):
            arrive(tile_messages(1, h, p))
            for f in (1, 0):
                start(tile_messages(2, h, p, f))
    for h in sets:
        for p in range(PARTS):
            pass_on(h, p).wait_send()
            sent = [early(1, h, p)] + [late(h, p, f) for f in range(3)]
            sent += [tile_messages(0, h, p), tile_messages(1, h, p)]
            for remotes, _ in sent:
                for copy in remotes:
                    copy.wait_send()
    for stage in range(3):
        for copy in label_messages(stage)[0]:
            copy.wait_send()
    for h in sets:
        keeps[h].wait()
        for p in range(PARTS):
            for f in (1, 0):
                arrive(tile_messages(2, h, p, f))
    for h in sets:
        for p in range(PARTS):
            for f in (1, 0):
                for copy in tile_messages(2, h, p, f)[0]:
                    copy.wait_send()


def sums_and_partners(cell, turn, labels, strength, freqs, collective_id):
    _, bands, _, trip = strength.shape
    torus = (SIDE, SIDE, SIDE)
    smem = pl.BlockSpec(memory_space=pltpu.SMEM)
    anywhere = pl.BlockSpec(memory_space=pl.ANY)
    label_rows = (*torus, 2, 1, 1, LANES)
    moving_labels = pltpu.VMEM(label_rows, jnp.int32)
    dma = pltpu.SemaphoreType.DMA
    slots = 4 * SIDE**3
    parts = [(PARTS, height, LANES) for height in HEIGHTS]

    def both(*front):
        return [(*front, *part) for part in parts]

    def moving(cores):
        return [(PARTS, cores, *torus, *part[1:]) for part in parts]

    buffers = [both(3, *torus), moving(3), moving(3), both(*torus), both(*torus), both(*torus, 2)]
    buffers += [moving(2), moving(2)]
    outs = both(2, *torus) + both(*torus, 2)
    return pl.pallas_call(
        main_kernel,
        name="sums_and_partners",
        out_shape=[jax.ShapeDtypeStruct(shape, jnp.bfloat16) for shape in outs]
        + [jax.ShapeDtypeStruct((1,), jnp.int32)],
        in_specs=[smem, smem, smem, anywhere, pl.BlockSpec(memory_space=pltpu.VMEM)],
        out_specs=[anywhere] * 4 + [smem],
        scratch_shapes=[
            pltpu.VMEM(strength.shape, strength.dtype),
            pltpu.VMEM((2 * trip + 1, bands, LANES), jnp.float32),
            pltpu.VMEM((2 * trip, 8, LANES), jnp.float32),
            *[pltpu.VMEM(shape, jnp.bfloat16) for pair in buffers for shape in pair],
            moving_labels,
            moving_labels,
            moving_labels,
            moving_labels,
            pltpu.SMEM(label_rows, jnp.int32),
            pltpu.VMEM((8, slots), jnp.int32),
            pltpu.SMEM((8, slots), jnp.int32),
            dma((PIECES,)),
            dma((2, 2, PARTS, SIDE, 3)),
            dma((2, 2, PARTS, SIDE, 3)),
            dma((2, 2, PARTS, SIDE)),
            dma((2, PARTS, 4, 4)),
            dma((2, PARTS, 4, 4)),
            dma((2, PARTS, 3)),
            dma((3, 7)),
            dma((3, 7)),
            dma((3,)),
            dma((3, 2, PARTS, 2, 4)),
            dma((3, 2, PARTS, 2, 4)),
            dma((3, 2, PARTS)),
            dma,
            dma((2,)),
        ],
        compiler_params=pltpu.CompilerParams(
            collective_id=collective_id, has_side_effects=True, vmem_limit_bytes=60 * 2**20
        ),
    )(cell, turn, labels, strength, freqs)


def sum_kernel(labels, one, two, out, total):
    step = pl.program_id(0)
    here = one.shape[0]
    tiles = out.shape[0]

    @pl.when(step == 0)
    def _():
        @pl.loop(0, tiles, unroll=4)
        def _(k):
            total[k] = jnp.zeros(total.shape[1:], jnp.float32)

    @pl.loop(0, here, unroll=4)
    def _(s):
        for r, got in enumerate((one, two)):
            label = labels[step * here + s, r]
            total[jnp.where(label < 0, tiles, label)] += got[s].astype(jnp.float32)

    @pl.when(step == pl.num_programs(0) - 1)
    def _():
        @pl.loop(0, tiles, unroll=4)
        def _(k):
            out[k] = total[k].astype(out.dtype)


def sum_tiles(labels, one, two, tiles):
    devices, *part = one.shape
    here = 32
    spec = pl.BlockSpec((here, *part), lambda i: (i, 0, 0, 0))
    return pl.pallas_call(
        sum_kernel,
        name="sum_tiles",
        grid=(devices // here,),
        out_shape=jax.ShapeDtypeStruct((tiles, *part), jnp.bfloat16),
        in_specs=[pl.BlockSpec(memory_space=pltpu.SMEM), spec, spec],
        out_specs=pl.BlockSpec(memory_space=pltpu.VMEM),
        scratch_shapes=[pltpu.VMEM((tiles + 1, *part), jnp.float32)],
        compiler_params=pltpu.CompilerParams(vmem_limit_bytes=VMEM_BYTES),
    )(labels, one, two)


def symmetrize_kernel(n, *refs):
    omegas, partners, out = refs[:n], refs[n : 2 * n], refs[2 * n]
    bands = out.shape[2]

    def whole(refs, at):
        pieces = [ref[at].astype(jnp.float32).reshape(-1, LANES) for ref in refs]
        return jnp.concatenate(pieces, axis=0)

    for z in range(SIDE):
        for core in range(2):
            for x in range(SIDE):
                mine = whole(omegas, (core, x, 0, z))
                other = whole(partners, (x, 0, z, core)).T
                out[z * 2 + core, pl.ds(x, bands, stride=SIDE), :] = 0.5 * (
                    mine[:, 0:bands] + other[0:bands]
                )


def symmetrize(omegas, partners):
    rests = [omega.shape[4:] for omega in omegas]
    bands = sum(rest[0] * rest[1] for rest in rests)
    rows = 2 * SIDE
    return pl.pallas_call(
        functools.partial(symmetrize_kernel, len(omegas)),
        name="symmetrize",
        grid=(SIDE,),
        out_shape=jax.ShapeDtypeStruct((rows * SIDE, bands * SIDE, bands), jnp.float32),
        in_specs=[
            pl.BlockSpec((2, SIDE, 1, SIDE, *rest), lambda y: (0, 0, y, 0, 0, 0, 0))
            for rest in rests
        ]
        + [
            pl.BlockSpec((SIDE, 1, SIDE, 2, *rest), lambda y: (0, y, 0, 0, 0, 0, 0))
            for rest in rests
        ],
        out_specs=pl.BlockSpec((rows, bands * SIDE, bands), lambda y: (y, 0, 0)),
        compiler_params=pltpu.CompilerParams(vmem_limit_bytes=60 * 2**20),
    )(*omegas, *partners)


def per_device(strength, freqs, owner, tile_slot, live_count):
    bands = strength.shape[2]
    n_grp = lax.axis_size("grp")
    n_dev = lax.axis_size("dev")
    grid = (n_grp, n_dev)
    devices = n_grp * n_dev
    part = (PARTS, bands // PARTS, LANES)
    torus = (SIDE, SIDE, SIDE)
    plain = ((0, 1, 2, 3), (0, 1, 2, 3))
    by_lane, freqs = strength.transpose(1, 2, 3, 0), freqs.transpose(1, 2, 0)
    names = (owner[:, 0], tile_slot, live_count)

    def with_labels(labels):
        return labels.reshape(*torus, 2, 1, 1, LANES)

    cell, turn, labels = make_plan(*names, grid)
    *halves, flag = sums_and_partners(
        cell, turn, labels, by_lane, freqs, 1
    )

    def main():
        return symmetrize(halves[:2], halves[2:])

    def dense():
        cells, labels = dense_blocks(by_lane, freqs, *names, grid)
        cells = cells.reshape(2, 2, *torus, *part)
        moved = ((1, 2, 3, 0), (0, 1, 2, 3))
        one, two, labels = exchange(
            [cells[0], cells[1], with_labels(labels)], [moved, moved, plain], 3, "send_dense"
        )
        omega = sum_tiles(
            labels.reshape(devices, LANES),
            one.reshape(devices, *part),
            two.reshape(devices, *part),
            devices,
        )
        omega = omega.reshape(SIDE, SIDE, 2, n_grp, *part).transpose(2, 3, 0, 1, 4, 5, 6)
        (partner,) = exchange([omega], [moved], 2, "send_tiles")
        return symmetrize([omega], [partner])

    sym = lax.cond(flag[0] > 0, dense, main)
    return sym.reshape(devices // n_grp, bands, n_grp, 1, bands)


def solution(mesh):
    return jax.shard_map(
        per_device,
        mesh=mesh,
        in_specs=(
            P(("grp", "dev"), None, None, None),
            P(("grp", "dev"), None, None),
            P(("grp", "dev"), None),
            P(("grp", "dev")),
            P(("grp", "dev")),
        ),
        out_specs=P("grp", None, None, "dev", None),
        check_vma=False,
    )
```

```python
import functools

import jax
import jax.numpy as jnp
from jax import lax
from jax.experimental import pallas as pl
from jax.experimental.pallas import tpu as pltpu
from jax.sharding import PartitionSpec as P

MESH = pl.DeviceIdType.MESH
LANES = 128
SIDE = 4
VMEM_BYTES = 56 * 2**20


PARTS = 3
WALK = 400
PIECES = 12
HEIGHTS = (24, 16)


def position():
    g, d = lax.axis_index("grp"), lax.axis_index("dev")
    return g, d // 8, lax.rem(d // 2, 4), lax.rem(d, 2)


def device_at(pos, axis, step, flip):
    at = list(pos)
    if step:
        at[axis] = lax.rem(pos[axis] + step, SIDE)
    if flip:
        at[3] = 1 - pos[3]
    return at[0], (at[1] * SIDE + at[2]) * 2 + at[3]


def exchange_kernel(plans, *refs):
    n = len(plans)
    srcs, dsts, firsts, seconds = (refs[k * n : (k + 1) * n] for k in range(4))
    send_sem, recv_sem, own_sem = refs[4 * n :]
    pos = position()
    steps = (1, 3, 2)

    barrier = pltpu.get_barrier_semaphore()
    greeted = [(a, r, f) for a in range(3) for r in (1, 2, 3) for f in (False, True)]
    greeted.append((0, 0, True))
    for a, r, f in greeted:
        pl.semaphore_signal(
            barrier, inc=1, device_id=device_at(pos, a, r, f), device_id_type=MESH
        )
    pl.semaphore_wait(barrier, len(greeted))

    def view(ref, places, front, p, axis, at, core):
        index = [slice(None)] * 4
        index[places[axis]] = at
        index[places[3]] = core
        return ref.at[(p,) + tuple(index)] if front else ref.at[tuple(index) + (p,)]

    def ends(stage, k, f, p, step):
        src_places, dst_places = plans[k]
        axis = (p + stage) % 3
        there = lax.rem(pos[axis] + step, SIDE) if step else pos[axis]
        core = (pos[3], 1 - pos[3])[f]
        source = view((srcs, firsts, seconds)[stage][k], src_places, stage > 0, p, axis, there, core)
        if stage < 2:
            target = view((firsts, seconds)[stage][k], src_places, True, p, axis, pos[axis], core)
        else:
            target = view(dsts[k], dst_places, False, p, axis, pos[axis], pos[3])
        return source, target

    def remote(stage, k, f, p, m):
        step = (*steps, 0)[m]
        source, target = ends(stage, k, f, p, step)
        return pltpu.make_async_remote_copy(
            src_ref=source,
            dst_ref=target,
            send_sem=send_sem.at[stage, k, f, p, m],
            recv_sem=recv_sem.at[stage, k, f, p, m],
            device_id=device_at(pos, (p + stage) % 3, step, stage == 2 and f == 1),
            device_id_type=MESH,
        )

    def copies(stage, k, f, p):
        if stage == 2 and f == 1:
            return [remote(stage, k, f, p, m) for m in range(4)], []
        source, target = ends(stage, k, f, p, 0)
        return (
            [remote(stage, k, f, p, m) for m in range(3)],
            [pltpu.make_async_copy(source, target, own_sem.at[stage, k, f, p])],
        )

    def start(*job):
        for group in copies(*job):
            for copy in group:
                copy.start()

    def arrive(*job):
        remotes, locals_ = copies(*job)
        for copy in remotes:
            copy.wait_recv()
        for copy in locals_:
            copy.wait()

    jobs = [
        (k, f, p)
        for f in (1, 0)
        for p in range(PARTS)
        for k in range(n)
        if p < firsts[k].shape[0]
    ]
    for job in jobs:
        start(0, *job)
    for stage in (1, 2):
        for job in jobs:
            arrive(stage - 1, *job)
            start(stage, *job)
    for job in jobs:
        arrive(2, *job)
    for stage in range(3):
        for job in jobs:
            for copy in copies(stage, *job)[0]:
                copy.wait_send()


def exchange(arrays, plans, collective_id, name):
    n = len(arrays)
    outs, temps = [], []
    for a, (src_places, dst_places) in zip(arrays, plans):
        front = [0] * 4
        for axis in range(4):
            front[dst_places[axis]] = a.shape[src_places[axis]]
        rest = a.shape[4:]
        outs.append(jax.ShapeDtypeStruct((*front, *rest), a.dtype))
        temps.append(pltpu.VMEM((rest[0],) + a.shape[:4] + rest[1:], a.dtype))
    anywhere = pl.BlockSpec(memory_space=pl.ANY)
    return pl.pallas_call(
        functools.partial(exchange_kernel, plans),
        name=name,
        out_shape=outs,
        in_specs=[anywhere] * n,
        out_specs=[anywhere] * n,
        scratch_shapes=temps
        + temps
        + [pltpu.SemaphoreType.DMA((3, n, 2, PARTS, 4))] * 2
        + [pltpu.SemaphoreType.DMA((3, n, 2, PARTS))],
        compiler_params=pltpu.CompilerParams(
            collective_id=collective_id, has_side_effects=True, vmem_limit_bytes=VMEM_BYTES
        ),
    )(*arrays)


def plan_kernel(grid, owner, tile, live, cell, turn, labels, left):
    n_grp, n_dev = grid
    devices = n_grp * n_dev
    chips = devices // 2

    @pl.loop(0, devices, unroll=8)
    def _(o):
        labels[0, o] = -1
        labels[1, o] = -1

    @pl.loop(0, cell.shape[0], unroll=8)
    def _(e):
        cell[e] = -1
        turn[e] = 0

    def first(t, n):
        o = owner[t]
        e = lax.rem(o, 2) * chips + lax.div(o, 2)
        held = cell[e]
        alive = t < live[0]
        taken = held >= 0
        kept = taken | jnp.logical_not(alive)
        cell[e] = jnp.where(kept, held, t)
        labels[0, o] = jnp.where(kept, labels[0, o], tile[t])
        left[n] = t
        return n + (taken & alive).astype(jnp.int32)

    n_left = lax.fori_loop(0, tile.shape[0], first, jnp.int32(0), unroll=8)

    def insert(q, carry):
        lost, noise = carry

        def body(state):
            t, steps, noise = state
            o, k = owner[t], tile[t]
            x = lax.rem(k, n_grp) * n_dev + lax.div(k, n_grp)
            e0 = lax.rem(o, 2) * chips + lax.div(o, 2)
            e1 = devices + lax.div(o, 2)
            e2 = lax.rem(x, 2) * chips + lax.div(x, 2)
            e3 = devices + lax.div(x, 2)
            noise = lax.rem(noise * 1103 + 12345, 65521)
            pick = lax.rem(lax.div(noise, 8), 4)
            for r, e in ((3, e3), (2, e2), (0, e0), (1, e1)):
                pick = jnp.where(cell[e] < 0, r, pick)
            e = jnp.where(pick == 0, e0, jnp.where(pick == 1, e1, jnp.where(pick == 2, e2, e3)))
            turned = pick >= 2
            to = jnp.where(turned, x, o)
            label = jnp.where(turned, lax.rem(o, n_dev) * n_grp + lax.div(o, n_dev), k)
            victim = cell[e]
            cell[e] = t
            turn[e] = turned.astype(jnp.int32)
            both = (e >= devices).astype(jnp.int32)
            labels[both, to] = label

            @pl.when(e >= devices)
            def _():
                labels[1, to + 1 - 2 * lax.rem(to, 2)] = -1

            return victim, steps + 1, noise

        t, _, noise = lax.while_loop(
            lambda state: (state[0] >= 0) & (state[1] < WALK), body, (left[q], 0, noise)
        )
        return lost | (t >= 0).astype(jnp.int32), noise

    lost, _ = lax.fori_loop(0, n_left, insert, (jnp.int32(0), jnp.int32(1)))

    labels[2, 0] = lost


def make_plan(owner, tile, live, grid):
    devices = grid[0] * grid[1]
    smem = pl.BlockSpec(memory_space=pltpu.SMEM)
    cells = jax.ShapeDtypeStruct((devices * 3 // 2,), jnp.int32)
    return pl.pallas_call(
        functools.partial(plan_kernel, grid),
        name="plan",
        out_shape=[cells, cells, jax.ShapeDtypeStruct((3, devices), jnp.int32)],
        in_specs=[smem] * 3,
        out_specs=[smem] * 3,
        scratch_shapes=[pltpu.SMEM((tile.shape[0] + 1,), jnp.int32)],
    )(owner, tile, live)


def fetch_copies(strength, here, in_sem):
    pieces = in_sem.shape[0]
    piece = strength.shape[1] // pieces
    return [
        pltpu.make_async_copy(
            strength.at[:, pl.ds(i * piece, piece)],
            here.at[:, pl.ds(i * piece, piece)],
            in_sem.at[i],
        )
        for i in range(pieces)
    ]


def turn_factors(fetches, freqs, here, turned, rows):
    _, bands, _, trip = here.shape
    flat = turned.reshape(turned.shape[0] * bands, LANES)
    flat_rows = rows.reshape(2 * trip * 8, LANES)
    lines = []
    for mode in (0, 1):
        occ = 1.0 / (jnp.exp(freqs[mode]) - 1.0)
        lines.append((freqs[mode].T, jnp.sqrt(occ * (occ + 1.0)).T))
    for f in (0, 1):
        for q, value in enumerate(lines[f] + lines[1 - f]):
            flat_rows[pl.ds(f * trip * 8 + q, trip, stride=8), 0:bands] = value
    third = 1.0 / (jnp.exp(freqs[2]) - 1.0) + 1.0
    eye = (
        lax.broadcasted_iota(jnp.int32, (trip, trip), 0)
        == lax.broadcasted_iota(jnp.int32, (trip, trip), 1)
    ).astype(jnp.bfloat16)
    piece = bands // len(fetches)
    for i, fetch in enumerate(fetches):
        fetch.wait()

        @pl.loop(i * piece, (i + 1) * piece, unroll=10)
        def _(j):
            scaled = (here[0, j].astype(jnp.float32) * third).astype(jnp.bfloat16)
            flat[pl.ds(j, trip, stride=bands), 0:bands] = scaled.T.astype(jnp.float32)
            other = lax.dot_general(
                eye, here[1, j], (((1,), (1,)), ((), ())), preferred_element_type=jnp.float32
            )
            flat[pl.ds(trip * bands + j, trip, stride=bands), 0:bands] = other


def block_of(turned, rows, trip, bands, t, f):
    factors = [
        turned[h * trip + t][:, 0:bands].astype(jnp.bfloat16) for h in (f, 1 - f)
    ]
    core = lax.dot_general(
        *factors, (((1,), (1,)), ((), ())), preferred_element_type=jnp.float32
    )
    line = rows[f * trip + t]
    column = line.T[0:bands]
    diff = column[:, 0:1] - line[2:3, 0:bands]
    scale = column[:, 1:2] * line[3:4, 0:bands] * jnp.exp(-diff * diff / 0.5)
    return jnp.pad(scale * core, ((0, 0), (0, LANES - bands)))


def dense_kernel(
    grid, owner, tile, live, strength, freqs, out, labels,
    here, turned, rows, block, cell, place, in_sem, out_sem,
):
    _, bands, _, trip = strength.shape
    devices = grid[0] * grid[1]
    chips = devices // 2
    fetches = fetch_copies(strength, here, in_sem)
    for fetch in fetches:
        fetch.start()

    @pl.loop(0, devices)
    def _(o):
        labels[o, 0] = -1
        labels[o, 1] = -1
        cell[o] = 0

    @pl.loop(0, trip)
    def _(t):
        place[t] = -1

    @pl.loop(0, live[0])
    def _(t):
        o = owner[t]
        r = cell[o]
        cell[o] = r + 1
        place[t] = (r * 2 + lax.rem(o, 2)) * chips + lax.div(o, 2)
        labels[o, r] = tile[t]

    turn_factors(fetches, freqs, here, turned, rows)

    def send(t):
        return pltpu.make_async_copy(block.at[t], out.at[place[t]], out_sem)

    @pl.loop(0, trip)
    def _(t):
        value = block_of(turned, rows, trip, bands, t, 0)
        block[t] = value.reshape(block.shape[1:]).astype(block.dtype)

        @pl.when(place[t] >= 0)
        def _():
            send(t).start()

    @pl.loop(0, trip)
    def _(t):
        @pl.when(place[t] >= 0)
        def _():
            send(t).wait()


def dense_blocks(strength, freqs, owner, tile, live, grid):
    _, bands, _, trip = strength.shape
    devices = grid[0] * grid[1]
    smem = pl.BlockSpec(memory_space=pltpu.SMEM)
    anywhere = pl.BlockSpec(memory_space=pl.ANY)
    part = (PARTS, bands // PARTS, LANES)
    return pl.pallas_call(
        functools.partial(dense_kernel, grid),
        name="dense_blocks",
        out_shape=[
            jax.ShapeDtypeStruct((devices * 2, *part), jnp.bfloat16),
            jax.ShapeDtypeStruct((devices, LANES), jnp.int32),
        ],
        in_specs=[smem, smem, smem, anywhere, pl.BlockSpec(memory_space=pltpu.VMEM)],
        out_specs=[anywhere, smem],
        scratch_shapes=[
            pltpu.VMEM(strength.shape, strength.dtype),
            pltpu.VMEM((2 * trip, bands, LANES), jnp.float32),
            pltpu.VMEM((2 * trip, 8, LANES), jnp.float32),
            pltpu.VMEM((trip, *part), jnp.bfloat16),
            pltpu.SMEM((devices,), jnp.int32),
            pltpu.SMEM((trip,), jnp.int32),
            pltpu.SemaphoreType.DMA((PIECES,)),
            pltpu.SemaphoreType.DMA,
        ],
        compiler_params=pltpu.CompilerParams(vmem_limit_bytes=VMEM_BYTES),
    )(owner, tile, live, strength, freqs)


def main_kernel(cell, turn, names, strength, freqs, *refs):
    omega_out, partner_out, refs = refs[:2], refs[2:4], refs[4:]
    flag, here, turned, rows, refs = *refs[:4], refs[4:]
    staged, first, second, got_same, got_other, got_shared, tile_first, tile_second = (
        refs[2 * r : 2 * r + 2] for r in range(8)
    )
    labels, labels_first, labels_second, labels_third, known, table, listed, *refs = refs[16:]
    in_sem, send_sem, recv_sem, own_sem, last_send, last_recv, last_own, *refs = refs
    labels_send, labels_recv, labels_own, tile_send, tile_recv, tile_own, small_sem, keep_sem = refs
    _, bands, _, trip = strength.shape
    pos = position()
    steps = (1, 3, 2)
    slabs = (1, 3, 2, 0)
    sets = (0, 1)
    fetches = fetch_copies(strength, here, in_sem)
    for fetch in fetches:
        fetch.start()

    barrier = pltpu.get_barrier_semaphore()
    greeted = [(a, r, f) for a in range(3) for r in (1, 2, 3) for f in (False, True)]
    greeted.append((0, 0, True))
    for a, r, f in greeted:
        pl.semaphore_signal(
            barrier, inc=1, device_id=device_at(pos, a, r, f), device_id_type=MESH
        )
    turn_factors(fetches, freqs, here, turned, rows)
    lane = lax.broadcasted_iota(jnp.int32, (1, LANES), 1)

    @pl.loop(0, 2 * SIDE**3, unroll=8)
    def _(o):
        known_here = jnp.where(lane == 0, names[0, o], jnp.where(lane == 1, names[1, o], names[2, 0]))
        labels[lax.div(o, 32), lax.rem(lax.div(o, 8), 4), lax.rem(lax.div(o, 2), 4), lax.rem(o, 2), 0] = (
            known_here
        )

    pl.semaphore_wait(barrier, len(greeted))

    def moved(axis, step):
        return lax.rem(pos[axis] + step, SIDE) if step else pos[axis]

    def compute(x):
        @pl.loop(0, 6)
        def _(i):
            k, half = lax.div(i, 2), lax.rem(i, 2)
            for u in range(8):
                e = k * SIDE**3 + x * SIDE**2 + half * 8 + u
                t = jnp.maximum(cell[e], 0)
                value = block_of(turned, rows, trip, bands, t, turn[e])
                begin = 0
                for h in sets:
                    shape = staged[h].shape[4:]
                    end = begin + shape[0] * shape[1]
                    staged[h][k, x, half * 2 + u // SIDE, u % SIDE] = (
                        value[begin:end].reshape(shape).astype(staged[h].dtype)
                    )
                    begin = end

    def cut(ref, front, p, core, **at):
        index = [core] + [at.get(name, slice(None)) for name in "xyz"]
        return ref.at[(p, *index)] if front else ref.at[(*index, p)]

    def early(stage, h, p, q=None):
        axis = (p + stage) % 3
        source, target = ((staged, first), (first, second))[stage]

        def ends(step):
            there, here_at = {"xyz"[axis]: moved(axis, step)}, {"xyz"[axis]: pos[axis]}
            if axis and q is not None:
                there["x"] = here_at["x"] = moved(0, slabs[q])
            return (
                cut(source[h], stage > 0, p, slice(None), **there),
                cut(target[h], True, p, slice(None), **here_at),
            )

        def remote(m, step):
            source_at, target_at = ends(step)
            at = (stage, h, p, q or 0, m)
            return pltpu.make_async_remote_copy(
                src_ref=source_at,
                dst_ref=target_at,
                send_sem=send_sem.at[at],
                recv_sem=recv_sem.at[at],
                device_id=device_at(pos, axis, step, False),
                device_id_type=MESH,
            )

        local = [pltpu.make_async_copy(*ends(0), own_sem.at[stage, h, p, q or 0])]
        if axis == 0 and q is not None:
            return ([remote(0, slabs[q])], []) if slabs[q] else ([], local)
        return [remote(m, step) for m, step in enumerate(steps)], local

    def late(h, p, f):
        axis = (p + 2) % 3
        core = (pos[3], 1 - pos[3], 2)[f]

        def ends(step):
            source = cut(second[h], True, p, core, **{"xyz"[axis]: moved(axis, step)})
            index = [slice(None)] * 3
            index[axis] = pos[axis]
            if f == 2:
                return source, got_shared[h].at[(*index, pos[3], p)]
            return source, (got_same, got_other)[f][h].at[(*index, p)]

        remotes = []
        for m, step in enumerate((*steps, 0) if f == 1 else steps):
            source, target = ends(step)
            remotes.append(
                pltpu.make_async_remote_copy(
                    src_ref=source,
                    dst_ref=target,
                    send_sem=last_send.at[h, p, f, m],
                    recv_sem=last_recv.at[h, p, f, m],
                    device_id=device_at(pos, axis, step, f == 1),
                    device_id_type=MESH,
                )
            )
        if f == 1:
            return remotes, []
        return remotes, [pltpu.make_async_copy(*ends(0), last_own.at[h, p, f])]

    def pass_on(h, p):
        mine = got_shared[h].at[:, :, :, pos[3], p]
        return pltpu.make_async_remote_copy(
            src_ref=mine,
            dst_ref=mine,
            send_sem=last_send.at[h, p, 3, 0],
            recv_sem=last_recv.at[h, p, 3, 0],
            device_id=device_at(pos, 0, 0, True),
            device_id_type=MESH,
        )

    def label_messages(stage):
        source, target = (
            (labels, labels_first), (labels_first, labels_second), (labels_second, labels_third)
        )[stage]
        moves = [(r, f) for r in steps for f in (False, True)[: 1 + stage // 2]]
        moves += [(0, True)] if stage == 2 else []

        def ends(step, flip):
            at = [slice(None)] * 4
            to = [slice(None)] * 4
            at[stage], to[stage] = moved(stage, step), pos[stage]
            if stage == 2:
                at[3], to[3] = 1 - pos[3] if flip else pos[3], pos[3]
            return source.at[tuple(at)], target.at[tuple(to)]

        remotes = []
        for m, (step, flip) in enumerate(moves):
            source_at, target_at = ends(step, flip)
            remotes.append(
                pltpu.make_async_remote_copy(
                    src_ref=source_at,
                    dst_ref=target_at,
                    send_sem=labels_send.at[stage, m],
                    recv_sem=labels_recv.at[stage, m],
                    device_id=device_at(pos, stage, step, flip),
                    device_id_type=MESH,
                )
            )
        return remotes, [pltpu.make_async_copy(*ends(0, False), labels_own.at[stage])]

    def start(messages):
        for group in messages:
            for copy in group:
                copy.start()

    def arrive(messages):
        remotes, locals_ = messages
        for copy in remotes:
            copy.wait_recv()
        for copy in locals_:
            copy.wait()

    def order_labels():
        copy = pltpu.make_async_copy(labels_third, known, small_sem)
        copy.start()
        copy.wait()
        sources = 2 * SIDE**3
        n = 2 * sources
        lanes = lax.broadcasted_iota(jnp.int32, (8, n), 1)

        def gather(s, carry):
            keys, bad = carry
            core = lax.rem(s, 2)
            at = (lax.div(s, 32), lax.rem(lax.div(s, 8), 4), lax.rem(lax.div(s, 2), 4), core, 0, 0)
            for r in range(2):
                label = known[(*at, r)]
                label = jnp.where(label < 0, sources, label)
                if r == 0:
                    label = label + jnp.where(core == pos[3], 2, 1) * (sources + 1)
                keys = jnp.where(lanes == s + r * sources, label, keys)
            return keys, jnp.maximum(bad, known[(*at, 2)])

        names_row, bad = lax.fori_loop(
            0, sources, gather, (jnp.zeros((8, n), jnp.int32), jnp.int32(0)), unroll=8
        )
        flag[0] = bad
        row = lax.broadcasted_iota(jnp.int32, (n, n), 0)
        column = lax.broadcasted_iota(jnp.int32, (n, n), 1)
        keys = names_row * n + lanes
        keys_down = keys.T[:, 0:1]
        names_down = names_row.T[:, 0:1]

        def count(mask):
            return jnp.sum(mask.astype(jnp.int32), axis=0, keepdims=True)

        ahead = keys_down < keys[0:1]
        rank = count(ahead)
        earlier = jnp.minimum(count(ahead & (names_down == names_row[0:1])), 1)
        both = jnp.concatenate([rank, earlier] + [rank] * 6, axis=0).T
        found = both[:, 0:1] == column
        index = jnp.where(row < sources, lax.shift_right_logical(row, 1), row - sources)
        table[0:1, :] = jnp.sum(jnp.where(found, index, 0), axis=0, keepdims=True)
        table[1:2, :] = jnp.sum(jnp.where(found, both[:, 1:2], 0), axis=0, keepdims=True)
        for g in range(3):
            name = column + g * (sources + 1)
            end = count(names_down <= name)
            begin = count(names_down < name)
            table[2 + g : 3 + g, :] = jnp.where(end > begin, end - 1, n)
        copy = pltpu.make_async_copy(table, listed, small_sem)
        copy.start()
        copy.wait()

    n_slots = 4 * SIDE**3
    sums = turned.reshape(n_slots + 1, bands // 8, 8, LANES)
    tile_rows = [staged[h].shape[4] * staged[h].shape[5] // 8 for h in sets]
    spans = [slice(0, tile_rows[0]), slice(tile_rows[0], sum(tile_rows))]

    def sum_group(h, got, begin, end):
        def add(r, total):
            kept = listed[1, r].astype(jnp.float32)
            at = listed[0, r]
            index = []
            for length in reversed(got.shape[:-3]):
                index.insert(0, jnp.bitwise_and(at, length - 1))
                at = lax.shift_right_logical(at, length.bit_length() - 1)
            block = got[tuple(index)].astype(jnp.float32).reshape(total.shape)
            total = total * kept + block
            sums[r, spans[h]] = total
            return total

        lax.fori_loop(
            begin, end, add, jnp.zeros((tile_rows[h], 8, LANES), jnp.float32), unroll=4
        )

    def sum_part(h, p):
        _, height, _ = staged[h].shape[4:]
        begin = spans[h].start + p * height // 8
        span = slice(begin, begin + height // 8)

        @pl.loop(0, n_slots // 2, unroll=8)
        def _(k):
            total = sums[listed[2, k]][span] + sums[listed[3, k]][span] + sums[listed[4, k]][span]
            x, d = lax.rem(k, SIDE), lax.div(k, SIDE)
            staged[h][lax.rem(d, 2), x, lax.div(d, 8), lax.rem(lax.div(d, 2), SIDE), p] = (
                total.reshape(height, LANES).astype(staged[h].dtype)
            )

    def tile_messages(stage, h, p, f=None):
        axis = (p + stage) % 3
        core = slice(0, 2) if f is None else (1 - pos[3] if f else pos[3])

        def ends(step):
            there, here_at = {"xyz"[axis]: moved(axis, step)}, {"xyz"[axis]: pos[axis]}
            source = cut((staged, tile_first, tile_second)[stage][h], stage > 0, p, core, **there)
            if stage < 2:
                return source, cut((tile_first, tile_second)[stage][h], True, p, core, **here_at)
            index = [here_at.get(name, slice(None)) for name in "xyz"]
            return source, partner_out[h].at[(*index, pos[3], p)]

        remotes = []
        for m, step in enumerate((*steps, 0) if f else steps):
            source, target = ends(step)
            at = (stage, h, p, f or 0, m)
            remotes.append(
                pltpu.make_async_remote_copy(
                    src_ref=source,
                    dst_ref=target,
                    send_sem=tile_send.at[at],
                    recv_sem=tile_recv.at[at],
                    device_id=device_at(pos, axis, step, bool(f)),
                    device_id_type=MESH,
                )
            )
        if f:
            return remotes, []
        return remotes, [pltpu.make_async_copy(*ends(0), tile_own.at[stage, h, p])]

    start(label_messages(0))
    for q in range(SIDE):
        compute(moved(0, slabs[q]))
        for p in range(PARTS):
            start(early(0, 0, p, q))
    for p in range(PARTS):
        start(early(0, 1, p))
    arrive(label_messages(0))
    start(label_messages(1))
    for p in range(PARTS):
        for q in range(SIDE):
            remotes, local = early(0, 0, p, q)
            arrive((remotes, local))
        start(early(1, 0, p))
    for p in range(PARTS):
        arrive(early(0, 1, p))
        start(early(1, 1, p))
    arrive(label_messages(1))
    start(label_messages(2))
    for h in sets:
        for p in range(PARTS):
            arrive(early(1, h, p))
            start(late(h, p, 2))
        for f in (1, 0):
            for p in range(PARTS):
                start(late(h, p, f))
    arrive(label_messages(2))
    order_labels()
    sums[n_slots] = jnp.zeros(sums.shape[1:], jnp.float32)
    keeps = [
        pltpu.make_async_copy(staged[h].at[0:2], omega_out[h], keep_sem.at[h]) for h in sets
    ]
    for h in sets:
        for p in range(PARTS):
            arrive(late(h, p, 2))
            pass_on(h, p).start()
        for p in range(PARTS):
            arrive(late(h, p, 1))
        sum_group(h, got_other[h], n_slots // 2, n_slots * 3 // 4)
        for p in range(PARTS):
            pass_on(h, p).wait_recv()
        sum_group(h, got_shared[h], 0, n_slots // 2)
        for p in range(PARTS):
            for q in [None] if h else range(SIDE):
                for copy in early(0, h, p, q)[0]:
                    copy.wait_send()
        for p in range(PARTS):
            arrive(late(h, p, 0))
        sum_group(h, got_same[h], n_slots * 3 // 4, n_slots)
        for p in range(PARTS):
            sum_part(h, p)
            start(tile_messages(0, h, p))
        keeps[h].start()
    for h in sets:
        for p in range(PARTS):
            arrive(tile_messages(0, h, p))
            start(tile_messages(1, h, p))
    for h in sets:
        for p in range(PARTS):
            arrive(tile_messages(1, h, p))
            for f in (1, 0):
                start(tile_messages(2, h, p, f))
    for h in sets:
        for p in range(PARTS):
            pass_on(h, p).wait_send()
            sent = [early(1, h, p)] + [late(h, p, f) for f in range(3)]
            sent += [tile_messages(0, h, p), tile_messages(1, h, p)]
            for remotes, _ in sent:
                for copy in remotes:
                    copy.wait_send()
    for stage in range(3):
        for copy in label_messages(stage)[0]:
            copy.wait_send()
    for h in sets:
        keeps[h].wait()
        for p in range(PARTS):
            for f in (1, 0):
                arrive(tile_messages(2, h, p, f))
    for h in sets:
        for p in range(PARTS):
            for f in (1, 0):
                for copy in tile_messages(2, h, p, f)[0]:
                    copy.wait_send()


def sums_and_partners(cell, turn, labels, strength, freqs, collective_id):
    _, bands, _, trip = strength.shape
    torus = (SIDE, SIDE, SIDE)
    smem = pl.BlockSpec(memory_space=pltpu.SMEM)
    anywhere = pl.BlockSpec(memory_space=pl.ANY)
    label_rows = (*torus, 2, 1, 1, LANES)
    moving_labels = pltpu.VMEM(label_rows, jnp.int32)
    dma = pltpu.SemaphoreType.DMA
    slots = 4 * SIDE**3
    parts = [(PARTS, height, LANES) for height in HEIGHTS]

    def both(*front):
        return [(*front, *part) for part in parts]

    def moving(cores):
        return [(PARTS, cores, *torus, *part[1:]) for part in parts]

    buffers = [both(3, *torus), moving(3), moving(3), both(*torus), both(*torus), both(*torus, 2)]
    buffers += [moving(2), moving(2)]
    outs = both(2, *torus) + both(*torus, 2)
    return pl.pallas_call(
        main_kernel,
        name="sums_and_partners",
        out_shape=[jax.ShapeDtypeStruct(shape, jnp.bfloat16) for shape in outs]
        + [jax.ShapeDtypeStruct((1,), jnp.int32)],
        in_specs=[smem, smem, smem, anywhere, pl.BlockSpec(memory_space=pltpu.VMEM)],
        out_specs=[anywhere] * 4 + [smem],
        scratch_shapes=[
            pltpu.VMEM(strength.shape, strength.dtype),
            pltpu.VMEM((2 * trip + 1, bands, LANES), jnp.float32),
            pltpu.VMEM((2 * trip, 8, LANES), jnp.float32),
            *[pltpu.VMEM(shape, jnp.bfloat16) for pair in buffers for shape in pair],
            moving_labels,
            moving_labels,
            moving_labels,
            moving_labels,
            pltpu.SMEM(label_rows, jnp.int32),
            pltpu.VMEM((8, slots), jnp.int32),
            pltpu.SMEM((8, slots), jnp.int32),
            dma((PIECES,)),
            dma((2, 2, PARTS, SIDE, 3)),
            dma((2, 2, PARTS, SIDE, 3)),
            dma((2, 2, PARTS, SIDE)),
            dma((2, PARTS, 4, 4)),
            dma((2, PARTS, 4, 4)),
            dma((2, PARTS, 3)),
            dma((3, 7)),
            dma((3, 7)),
            dma((3,)),
            dma((3, 2, PARTS, 2, 4)),
            dma((3, 2, PARTS, 2, 4)),
            dma((3, 2, PARTS)),
            dma,
            dma((2,)),
        ],
        compiler_params=pltpu.CompilerParams(
            collective_id=collective_id, has_side_effects=True, vmem_limit_bytes=60 * 2**20
        ),
    )(cell, turn, labels, strength, freqs)


def sum_kernel(labels, one, two, out, total):
    step = pl.program_id(0)
    here = one.shape[0]
    tiles = out.shape[0]

    @pl.when(step == 0)
    def _():
        @pl.loop(0, tiles, unroll=4)
        def _(k):
            total[k] = jnp.zeros(total.shape[1:], jnp.float32)

    @pl.loop(0, here, unroll=4)
    def _(s):
        for r, got in enumerate((one, two)):
            label = labels[step * here + s, r]
            total[jnp.where(label < 0, tiles, label)] += got[s].astype(jnp.float32)

    @pl.when(step == pl.num_programs(0) - 1)
    def _():
        @pl.loop(0, tiles, unroll=4)
        def _(k):
            out[k] = total[k].astype(out.dtype)


def sum_tiles(labels, one, two, tiles):
    devices, *part = one.shape
    here = 32
    spec = pl.BlockSpec((here, *part), lambda i: (i, 0, 0, 0))
    return pl.pallas_call(
        sum_kernel,
        name="sum_tiles",
        grid=(devices // here,),
        out_shape=jax.ShapeDtypeStruct((tiles, *part), jnp.bfloat16),
        in_specs=[pl.BlockSpec(memory_space=pltpu.SMEM), spec, spec],
        out_specs=pl.BlockSpec(memory_space=pltpu.VMEM),
        scratch_shapes=[pltpu.VMEM((tiles + 1, *part), jnp.float32)],
        compiler_params=pltpu.CompilerParams(vmem_limit_bytes=VMEM_BYTES),
    )(labels, one, two)


def symmetrize_kernel(n, *refs):
    omegas, partners, out = refs[:n], refs[n : 2 * n], refs[2 * n]
    bands = out.shape[2]

    def whole(refs, at):
        pieces = [ref[at].astype(jnp.float32).reshape(-1, LANES) for ref in refs]
        return jnp.concatenate(pieces, axis=0)

    for z in range(SIDE):
        for core in range(2):
            for x in range(SIDE):
                mine = whole(omegas, (core, x, 0, z))
                other = whole(partners, (x, 0, z, core)).T
                out[z * 2 + core, pl.ds(x, bands, stride=SIDE), :] = 0.5 * (
                    mine[:, 0:bands] + other[0:bands]
                )


def symmetrize(omegas, partners):
    rests = [omega.shape[4:] for omega in omegas]
    bands = sum(rest[0] * rest[1] for rest in rests)
    rows = 2 * SIDE
    return pl.pallas_call(
        functools.partial(symmetrize_kernel, len(omegas)),
        name="symmetrize",
        grid=(SIDE,),
        out_shape=jax.ShapeDtypeStruct((rows * SIDE, bands * SIDE, bands), jnp.float32),
        in_specs=[
            pl.BlockSpec((2, SIDE, 1, SIDE, *rest), lambda y: (0, 0, y, 0, 0, 0, 0))
            for rest in rests
        ]
        + [
            pl.BlockSpec((SIDE, 1, SIDE, 2, *rest), lambda y: (0, y, 0, 0, 0, 0, 0))
            for rest in rests
        ],
        out_specs=pl.BlockSpec((rows, bands * SIDE, bands), lambda y: (y, 0, 0)),
        compiler_params=pltpu.CompilerParams(vmem_limit_bytes=60 * 2**20),
    )(*omegas, *partners)


def per_device(strength, freqs, owner, tile_slot, live_count):
    bands = strength.shape[2]
    n_grp = lax.axis_size("grp")
    n_dev = lax.axis_size("dev")
    grid = (n_grp, n_dev)
    devices = n_grp * n_dev
    part = (PARTS, bands // PARTS, LANES)
    torus = (SIDE, SIDE, SIDE)
    plain = ((0, 1, 2, 3), (0, 1, 2, 3))
    by_lane, freqs = strength.transpose(1, 2, 3, 0), freqs.transpose(1, 2, 0)
    names = (owner[:, 0], tile_slot, live_count)

    def with_labels(labels):
        return labels.reshape(*torus, 2, 1, 1, LANES)

    cell, turn, labels = make_plan(*names, grid)
    *halves, flag = sums_and_partners(
        cell, turn, labels, by_lane, freqs, 1
    )

    def main():
        return symmetrize(halves[:2], halves[2:])

    def dense():
        cells, labels = dense_blocks(by_lane, freqs, *names, grid)
        cells = cells.reshape(2, 2, *torus, *part)
        moved = ((1, 2, 3, 0), (0, 1, 2, 3))
        one, two, labels = exchange(
            [cells[0], cells[1], with_labels(labels)], [moved, moved, plain], 3, "send_dense"
        )
        omega = sum_tiles(
            labels.reshape(devices, LANES),
            one.reshape(devices, *part),
            two.reshape(devices, *part),
            devices,
        )
        omega = omega.reshape(SIDE, SIDE, 2, n_grp, *part).transpose(2, 3, 0, 1, 4, 5, 6)
        (partner,) = exchange([omega], [moved], 2, "send_tiles")
        return symmetrize([omega], [partner])

    sym = lax.cond(flag[0] > 0, dense, main)
    return sym.reshape(devices // n_grp, bands, n_grp, 1, bands)


def solution(mesh):
    return jax.shard_map(
        per_device,
        mesh=mesh,
        in_specs=(
            P(("grp", "dev"), None, None, None),
            P(("grp", "dev"), None, None),
            P(("grp", "dev"), None),
            P(("grp", "dev")),
            P(("grp", "dev")),
        ),
        out_specs=P("grp", None, None, "dev", None),
        check_vma=False,
    )
```
